32 devices in a mesh: req: 4 (over x, core), exp: 8 (over z, y).
Axes of the slice: x: 2, y: 2, z: 4, core: 2. Of those that a mesh axis runs over, the one named last changes fastest.
Arguments:
- tokens: bfloat16 [2048, 2048], P(('req', 'exp')), may hold values from -6 to 6
- routes: int32 [2048, 2], P(('req', 'exp')), may hold values from 0 to 7, all different within a row; in each aligned block of 64 rows (0 to 63, 64 to 127, ...) at most 24 rows name the same one
- router: bfloat16 [2048, 8], replicated, may hold values from -0.26367188 to 0.26367188
- gate_weight: bfloat16 [2048, 90112], P(None, ('req', 'exp')), as said below
- up_weight: bfloat16 [2048, 90112], P(None, ('req', 'exp')), as said below
- down_weight: bfloat16 [90112, 2048], P(('req', 'exp')), as said below
- norm_gain: float32 [2048], replicated, may hold values from 0.5 to 1.5
- head_weight: bfloat16 [2048, 32000], P(None, 'exp'), may hold values from -0.39648438 to 0.39648438
- lengths: int32 [32, 4], P(('req', 'exp')), may hold values from 1 to 32, 64 in all within a row
Outputs:
- hidden_out: bfloat16 [2048, 2048], P(('req', 'exp'))
- request_norm: float32 [128], P(('req', 'exp'))
- request_max: float32 [128], P(('req', 'exp'))
The draws below stay inside these ranges and needn't reach their ends.
Inputs may be any that keep to these rules, and one draw needn't show every extreme that they name: `routes`: within a row the two experts differ. In each aligned block of 64 rows (the rows of one device) no expert is named by more than 24 rows. Each device's 4 lengths sum to 64. `gate_weight`: the two copies are equal, as the steps say. `up_weight`: the two copies are equal, as the steps say. `down_weight`: the two copies are equal, as the steps say.
All inputs are finite; a program needn't handle non-finite values.
Results may differ from the reference program's by a relative error of at most 0.0036.
Values may be sent and summed in bfloat16 or wider, within the bound.
No kernel may reach another device: no remote copies, remote signals or barrier semaphores. Data moves between devices by JAX's collectives and lax.ppermute only.
A program may use at most 128 MiB of HBM per device.

```python
import math
import jax
import jax.numpy as jnp
import numpy as np
from jax import lax

D = 2048
FF = 5632
EXPERTS = 8
VOCAB = 32000
TOK_DEV = 64
REQ_DEV = 4
CAP = 24
SLICE = 2816
TOKENS = 2048
N_REQ = 4
N_EXP = 8


def doubled_columns(key, salt):
    base = jax.random.normal(jax.random.fold_in(key, salt), (D, EXPERTS * FF), jnp.float32)
    base = jnp.clip(base, -6.0, 6.0) * D ** (-0.5)
    shaped = base.reshape(D, N_REQ, 1, N_EXP // 2, SLICE)
    both = jnp.broadcast_to(shaped, (D, N_REQ, 2, N_EXP // 2, SLICE))
    return both.reshape(D, 2 * EXPERTS * FF).astype(jnp.bfloat16)


def draw_gate_weight(key, part):
    return doubled_columns(key, 101)


def draw_up_weight(key, part):
    return doubled_columns(key, 202)


def draw_down_weight(key, part):
    base = jax.random.normal(jax.random.fold_in(key, 303), (EXPERTS * FF, D), jnp.float32)
    base = jnp.clip(base, -6.0, 6.0) * FF ** (-0.5)
    shaped = base.reshape(N_REQ, 1, N_EXP // 2, SLICE, D)
    both = jnp.broadcast_to(shaped, (N_REQ, 2, N_EXP // 2, SLICE, D))
    return both.reshape(2 * EXPERTS * FF, D).astype(jnp.bfloat16)


def shard_levels(own_key, shape, cuts, smallest, top_value):
    def one(axis_at, parts):
        draws = jax.random.uniform(jax.random.fold_in(jax.random.fold_in(own_key, 6), axis_at), (parts,), jnp.float32, smallest / len(cuts), top_value / len(cuts))
        return jnp.repeat(jnp.exp(draws), shape[axis_at] // parts).reshape((-1,) + (1,) * (len(shape) - axis_at - 1))

    factor_of = one(*cuts[0])
    for cut in cuts[1:]:
        factor_of = factor_of * one(*cut)
    return factor_of


def length_profile(amount, total, most, skew):
    loads = [(1 << 20) // math.isqrt(grade ** skew) + 1 for grade in range(2, amount + 1)]
    surplus, given = total - most - (amount - 1), [1] * (amount - 1)
    while surplus > 0:
        candidates = [i for i in range(amount - 1) if given[i] < most]
        whole, remaining = sum([loads[i] for i in candidates]), surplus
        for i in candidates:
            more = min(most - given[i], max(1, remaining * loads[i] // whole), surplus)
            given[i] = given[i] + more
            surplus = surplus - more
    return np.array([most] + given)


def uneven_parts(own_key, number_of, total, bound, skew):
    if number_of == 2:
        one = jax.random.randint(own_key, (), max(1, total - bound), min(bound, total - 1) + 1)
        return jnp.stack([one, total - one])
    sizes = jnp.asarray(length_profile(number_of, total, bound, skew), jnp.int32)
    pairs = (number_of - 1) // 2
    giver, taker = sizes[1:1 + 2 * pairs:2], sizes[2:2 + 2 * pairs:2]
    room = jnp.minimum(giver - 1, bound - taker)
    passed = jax.random.randint(jax.random.fold_in(own_key, 1), (pairs,), 0, 1 << 20) % (room + 1)
    sizes = sizes.at[1:1 + 2 * pairs:2].set(giver - passed).at[2:2 + 2 * pairs:2].set(taker + passed)
    return sizes[jax.random.permutation(jax.random.fold_in(own_key, 2), number_of)]


def shared_out(own_key, own, number, rows, number_of, top, bound, slope):
    sequence = jax.random.permutation(own_key, number_of)
    packed, usual = load_shares(number_of, rows * top, bound, slope, True), load_shares(number_of, rows * top, bound, slope, False)
    places = jnp.arange(number_of)

    def named(sizes, turn):
        used = int((sizes > 0).sum())
        fixed = max(1, used // 4)
        shifted = fixed + (places - fixed + turn * (used - fixed)) % max(1, number_of - fixed)
        return jnp.zeros((number_of,), jnp.int32).at[sequence[jnp.where(places < fixed, places, shifted)]].set(jnp.asarray(sizes, jnp.int32))

    sizes = jnp.where(number % 4 == 0, named(packed, number // 4), named(usual, number - number // 4 - 1))
    mixed = jax.random.permutation(jax.random.fold_in(own, 3), number_of)
    giver, sink = mixed[0:number_of // 2 * 2:2], mixed[1:number_of // 2 * 2:2]
    room = jnp.minimum(sizes[giver] - 1, bound - sizes[sink]) // 2
    room = jnp.where((giver == sequence[0]) | (sink == sequence[0]) | (sizes[sink] == 0), 0, jnp.maximum(room, 0))
    shifted = jax.random.randint(jax.random.fold_in(own, 4), (number_of // 2,), 0, 1 << 20) % (room + 1)
    sizes = sizes.at[giver].add(-shifted).at[sink].add(shifted)
    items = jnp.searchsorted(jnp.cumsum(sizes), jnp.arange(rows * top), side="right").astype(jnp.int32)
    table = items.reshape(top, rows).T
    table = table[jax.random.permutation(jax.random.fold_in(own, 1), rows)]
    turn = jax.random.randint(jax.random.fold_in(own, 2), (rows, 1), 0, top)
    return jnp.take_along_axis(table, (jnp.arange(top)[None, :] + turn) % top, axis=1)


def load_shares(number_of, total, limit, lean, full):
    loads = [(1 << 20) // math.isqrt(standing ** lean) + 1 for standing in range(1, number_of + 1)]
    largest = limit if full else min(limit, max(-(-total // number_of), total * loads[0] // sum(loads)))
    least = 1 if total - largest >= number_of - 1 else 0
    counts, spare = [largest] + [least] * (number_of - 1), total - largest - least * (number_of - 1)
    while spare > 0:
        candidates = [i for i in range(1, number_of) if counts[i] < largest] or [i for i in range(1, number_of) if counts[i] < limit]
        pool, left = sum([loads[i] for i in candidates]), spare
        for i in candidates:
            extra = min(limit - counts[i], max(1, left * loads[i] // pool), spare)
            counts[i] = counts[i] + extra
            spare = spare - extra
    return np.array(counts)


def scatter_about(key, shape, scale, reach, shards=(), kind=jnp.bfloat16):
    result = scale * jax.random.normal(key, shape, jnp.float32)
    if shards:
        result = result * shard_levels(key, shape, shards, -0.22, 0.18)
    return jnp.clip(result, -reach, reach).astype(kind)


def setup_inputs(seed: int = 0) -> dict:
    key_list = jax.random.split(jax.random.key(seed), 10)
    tokens = scatter_about(key_list[0], (TOKENS, D), 1.0, 6.0, ((0, 32),))
    routes_keys = jax.random.split(jax.random.fold_in(key_list[1], 1), TOKENS // TOK_DEV)
    routes_turns = jax.random.permutation(jax.random.fold_in(key_list[1], 3), TOKENS // TOK_DEV)
    routes = jax.vmap(lambda own, number: shared_out(jax.random.fold_in(key_list[1], 2), own, number, TOK_DEV, EXPERTS, 2, CAP, 2))(routes_keys, routes_turns).reshape((TOKENS, 2))
    router = scatter_about(key_list[2], (D, EXPERTS), (2.0 * D ** -0.5), 0.26367188)
    gate_weight = draw_gate_weight(jax.random.fold_in(key_list[9], 71), 0)
    up_weight = draw_up_weight(jax.random.fold_in(key_list[9], 71), 0)
    down_weight = draw_down_weight(jax.random.fold_in(key_list[9], 71), 0)
    norm_gain = jnp.clip(1.0 + 0.1 * jax.random.normal(key_list[6], (D,), jnp.float32), 0.5, 1.5)
    head_weight = scatter_about(key_list[7], (D, VOCAB), (3.0 * D ** -0.5), 0.39648438, ((1, 8),))
    lengths = jax.vmap(lambda own: uneven_parts(own, REQ_DEV, TOK_DEV, TOK_DEV // 2, 2))(jax.random.split(key_list[8], (N_REQ * N_EXP))).reshape((N_REQ * N_EXP, REQ_DEV)).astype(jnp.int32)
    return dict(tokens=tokens, routes=routes, router=router, gate_weight=gate_weight, up_weight=up_weight, down_weight=down_weight, norm_gain=norm_gain, head_weight=head_weight, lengths=lengths)


norm_eps = 1e-05

def expert_apply(routed_rows, w_gate, w_up, w_down):
    gate_act = jnp.dot(routed_rows, w_gate, preferred_element_type=jnp.float32)
    up_act = jnp.dot(routed_rows, w_up, preferred_element_type=jnp.float32)
    hidden = (jax.nn.silu(gate_act) * up_act).astype(jnp.bfloat16)
    return jnp.dot(hidden, w_down, preferred_element_type=jnp.float32)

def first_copy_columns(weight):
    width = weight.shape[0]
    shaped = weight.reshape(width, N_REQ, 2, N_EXP // 2, SLICE)
    return shaped[:, :, 0].reshape(width, EXPERTS * FF)

def first_copy_rows(weight):
    width = weight.shape[1]
    shaped = weight.reshape(N_REQ, 2, N_EXP // 2, SLICE, width)
    return shaped[:, 0].reshape(EXPERTS * FF, width)

def reference(tokens, routes, router, gate_weight, up_weight, down_weight, norm_gain, head_weight, lengths):
    gate_all = first_copy_columns(gate_weight)
    up_all = first_copy_columns(up_weight)
    down_all = first_copy_rows(down_weight)
    devices = lengths.shape[0]
    row_count = tokens.shape[0] // devices
    experts = router.shape[1]
    chosen_ids = routes.reshape(devices, row_count * 2).astype(jnp.int32)
    onehot = (chosen_ids[:, :, None] == jnp.arange(experts, dtype=jnp.int32)[None, None, :]).astype(jnp.int32)
    slot_rank = lax.optimization_barrier(jnp.sum((jnp.cumsum(onehot, axis=1).astype(jnp.int32) - 1) * onehot, axis=2)).astype(jnp.int32)
    slot_index = (jnp.arange(devices, dtype=jnp.int32)[:, None] * CAP + slot_rank).reshape(-1)
    expert_ids = chosen_ids.reshape(-1)
    row_id = (jnp.arange(devices * row_count * 2, dtype=jnp.int32) // 2).astype(jnp.int32)
    slot_table = jnp.full((experts, devices * CAP), -1, jnp.int32).at[expert_ids, slot_index].set(row_id)

    def run_expert(expert):
        slot_ids = slot_table[expert]
        routed_rows = jnp.where((slot_ids >= 0)[:, None], tokens[jnp.maximum(slot_ids, 0)], jnp.zeros((), tokens.dtype))
        w_gate = lax.dynamic_slice_in_dim(gate_all, expert * FF, FF, 1)
        w_up = lax.dynamic_slice_in_dim(up_all, expert * FF, FF, 1)
        w_down = lax.dynamic_slice_in_dim(down_all, expert * FF, FF, 0)
        return expert_apply(routed_rows, w_gate, w_up, w_down)
    expert_out = lax.map(run_expert, jnp.arange(experts, dtype=jnp.int32))
    picked = expert_out[expert_ids, slot_index].reshape(devices * row_count, 2, D)
    gating = jax.nn.sigmoid(jnp.dot(tokens, router, preferred_element_type=jnp.float32))
    chosen = jnp.take_along_axis(gating, routes, axis=1)
    branch_sum = lax.optimization_barrier(jnp.sum(chosen[:, :, None] * picked, axis=1))
    hidden_out = (tokens.astype(jnp.float32) + branch_sum).astype(jnp.bfloat16)
    widened = hidden_out.astype(jnp.float32)
    row_sq = lax.optimization_barrier(jnp.sum(widened * widened, axis=1))
    normed = (widened * lax.rsqrt(row_sq / D + norm_eps)[:, None] * norm_gain[None, :]).astype(jnp.bfloat16)

    def block_max(block_rows):
        return lax.optimization_barrier(jnp.max(jnp.dot(block_rows, head_weight, preferred_element_type=jnp.float32), axis=1))
    row_max = lax.map(block_max, normed.reshape(devices, row_count, D))
    request_ends = jnp.cumsum(lengths, axis=1).astype(jnp.int32)
    position = jnp.arange(row_count, dtype=jnp.int32)
    request_of = lax.optimization_barrier(jnp.sum((position[None, :, None] >= request_ends[:, None, :]).astype(jnp.int32), axis=2))
    member = request_of[:, :, None] == jnp.arange(lengths.shape[1], dtype=jnp.int32)[None, None, :]
    request_sq = lax.optimization_barrier(jnp.sum(jnp.where(member, row_sq.reshape(devices, row_count)[:, :, None], jnp.float32(0.0)), axis=1))
    request_norm = jnp.sqrt(request_sq / (lengths.astype(jnp.float32) * D))
    request_max = lax.optimization_barrier(jnp.max(jnp.where(member, row_max[:, :, None], jnp.float32(-jnp.inf)), axis=1))
    return (hidden_out, request_norm.reshape(-1), request_max.reshape(-1))
```

```python
import functools

import jax
import jax.numpy as jnp
from jax import lax
from jax.experimental import pallas as pl
from jax.experimental.pallas import tpu as pltpu
from jax.sharding import PartitionSpec as P

CAP = 24
META = 128
VMEM_LIMIT = 60 * 1024 * 1024

norm_eps = 1e-05
AXES = ("req", "exp")
F32 = jnp.float32
BF16 = jnp.bfloat16


def flip_pairs(n_req, n_exp, dim_of_core):
    pairs = []
    for r in range(n_req):
        for e in range(n_exp):
            flips = dim_of_core[r & 1]
            pr, pe = r, e
            for axis, bit in flips:
                if axis == "req":
                    pr ^= bit
                else:
                    pe ^= bit
            pairs.append((r * n_exp + e, pr * n_exp + pe))
    return pairs


def bits_below(n, first=1):
    out = []
    b = first
    while b < n:
        out.append(b)
        b *= 2
    return out


def prepare_kernel(tokens_ref, routes_ref, router_ref, out_ref):
    width = tokens_ref.shape[1]
    rows = tokens_ref.shape[0]
    t = tokens_ref[...]
    out_ref[:, :width] = t
    gating = 1.0 / (1.0 + jnp.exp(-jnp.dot(t, router_ref[...], preferred_element_type=F32)))
    routes = routes_ref[...]
    lane = lax.broadcasted_iota(jnp.int32, (rows, META), 1)
    expert = lax.broadcasted_iota(jnp.int32, gating.shape, 1)
    meta = jnp.zeros((rows, META), F32)
    for k in range(2):
        ids = routes[:, k : k + 1]
        chosen = jnp.sum(jnp.where(expert == ids, gating, 0.0), axis=1, keepdims=True)
        high = chosen.astype(BF16).astype(F32)
        mid = (chosen - high).astype(BF16).astype(F32)
        low = chosen - high - mid
        for j, piece in enumerate((ids.astype(F32), high, mid, low)):
            meta = jnp.where(lane == 4 * k + j, piece, meta)
    out_ref[:, width:] = meta.astype(BF16)


def prepare(tokens, routes, router):
    rows, width = tokens.shape
    return pl.pallas_call(
        prepare_kernel,
        out_shape=jax.ShapeDtypeStruct((rows, width + META), BF16),
        name="prepare",
    )(tokens, routes, router)


def expert_kernel(blocks, slots, expert_ref, *refs):
    block_refs = refs[:blocks]
    gate_ref, up_ref, down_ref = refs[blocks : blocks + 3]
    half = blocks // 2
    own_refs = refs[blocks + 3 : blocks + 3 + half]
    other_ref = refs[blocks + 3 + half]
    table, place, routed, scale, total, sems = refs[blocks + 4 + half :]
    rows = block_refs[0].shape[0]
    width = gate_ref.shape[0]
    count = blocks * rows
    step = pl.program_id(0)

    @pl.when(step == 0)
    def _():
        copies = [
            pltpu.make_async_copy(ref, table.at[pl.ds(i * rows, rows)], sems.at[i])
            for i, ref in enumerate(block_refs)
        ]
        for c in copies:
            c.start()
        for c in copies:
            c.wait()
        meta = table[:, width:].astype(F32)
        own = expert_ref[0].astype(F32)
        lane = lax.broadcasted_iota(jnp.int32, meta.shape, 1)
        first = meta[:, 0:1] == own
        second = meta[:, 4:5] == own
        member = jnp.logical_or(first, second)
        gate = jnp.where(
            first,
            meta[:, 1:2] + meta[:, 2:3] + meta[:, 3:4],
            meta[:, 5:6] + meta[:, 6:7] + meta[:, 7:8],
        )
        flags = jnp.where(jnp.logical_and(lane == 0, member), 1.0, 0.0).astype(BF16)
        before = lax.broadcasted_iota(jnp.int32, (count, count), 0) > lax.broadcasted_iota(
            jnp.int32, (count, count), 1
        )
        rank = jnp.dot(
            jnp.where(before, 1.0, 0.0).astype(BF16), flags, preferred_element_type=F32
        )[:, 0:1].astype(jnp.int32)
        slot = lax.broadcasted_iota(jnp.int32, (count, slots), 1)
        chosen = jnp.logical_and(slot == rank, member)
        place[...] = jnp.where(chosen, 1.0, 0.0).astype(BF16)
        scale[...] = jnp.transpose(
            jnp.broadcast_to(
                jnp.sum(jnp.where(chosen, gate, 0.0), axis=0, keepdims=True), (128, slots)
            )
        )
        routed[...] = lax.dot_general(
            place[...], table[:, :width], (((0,), (0,)), ((), ())), preferred_element_type=F32
        ).astype(BF16)

    x = routed[...]
    g = jnp.dot(x, gate_ref[...], preferred_element_type=F32)
    u = jnp.dot(x, up_ref[...], preferred_element_type=F32)
    hidden = (g / (1.0 + jnp.exp(-g)) * u).astype(BF16)
    y = jnp.dot(hidden, down_ref[...], preferred_element_type=F32)

    @pl.when(step == 0)
    def _():
        total[...] = y

    @pl.when(step > 0)
    def _():
        total[...] += y

    @pl.when(step == pl.num_programs(0) - 1)
    def _():
        weighted = (total[...] * scale[:, 0:1]).astype(BF16)
        for i, ref in enumerate(own_refs):
            ref[...] = jnp.dot(
                place[i * rows : (i + 1) * rows, :], weighted, preferred_element_type=F32
            ).astype(BF16)
        other_ref[...] = jnp.dot(
            place[half * rows :, :], weighted, preferred_element_type=F32
        ).astype(BF16)


def tile_of(size, want):
    for t in range(want, 0, -128):
        if size % t == 0:
            return t
    return size


def run_expert(expert, block_list, gate_weight, up_weight, down_weight, cap):
    blocks = len(block_list)
    rows = block_list[0].shape[0]
    width, hidden = gate_weight.shape
    half = blocks // 2
    slots = blocks * cap
    count = blocks * rows
    tile = tile_of(hidden, 256)
    whole = pl.BlockSpec(memory_space=pl.ANY)
    return pl.pallas_call(
        functools.partial(expert_kernel, blocks, slots),
        grid=(hidden // tile,),
        in_specs=[pl.BlockSpec(memory_space=pltpu.SMEM)]
        + [whole] * blocks
        + [
            pl.BlockSpec((width, tile), lambda i: (0, i)),
            pl.BlockSpec((width, tile), lambda i: (0, i)),
            pl.BlockSpec((tile, width), lambda i: (i, 0)),
        ],
        out_specs=[pl.BlockSpec((rows, width), lambda i: (0, 0))] * half
        + [pl.BlockSpec((half * rows, width), lambda i: (0, 0))],
        out_shape=[jax.ShapeDtypeStruct((rows, width), BF16)] * half
        + [jax.ShapeDtypeStruct((half * rows, width), BF16)],
        scratch_shapes=[
            pltpu.VMEM((count, width + META), BF16),
            pltpu.VMEM((count, slots), BF16),
            pltpu.VMEM((slots, width), BF16),
            pltpu.VMEM((slots, 128), F32),
            pltpu.VMEM((slots, width), F32),
            pltpu.SemaphoreType.DMA((blocks,)),
        ],
        compiler_params=pltpu.CompilerParams(
            vmem_limit_bytes=VMEM_LIMIT, dimension_semantics=("arbitrary",)
        ),
        cost_estimate=pl.CostEstimate(
            flops=6 * slots * width * hidden + 4 * slots * count * width,
            bytes_accessed=6 * width * hidden + 4 * count * width,
            transcendentals=slots * hidden,
        ),
        name="expert",
    )(expert, *block_list, gate_weight, up_weight, down_weight)


def finish_kernel(parts, tokens_ref, gain_ref, *refs):
    hidden_ref, normed_ref, square_ref = refs[parts:]
    total = refs[0][...].astype(F32)
    for ref in refs[1:parts]:
        total = total + ref[...].astype(F32)
    hidden = (tokens_ref[...].astype(F32) + total).astype(BF16)
    hidden_ref[...] = hidden
    wide = hidden.astype(F32)
    square = jnp.sum(wide * wide, axis=1, keepdims=True)
    normed_ref[...] = (
        wide * lax.rsqrt(square / wide.shape[1] + norm_eps) * gain_ref[...]
    ).astype(BF16)
    square_ref[...] = jnp.transpose(jnp.broadcast_to(square, (square.shape[0], 128)))[0:8, :]


def finish(tokens, gain, parts):
    rows, width = tokens.shape
    return pl.pallas_call(
        functools.partial(finish_kernel, len(parts)),
        out_shape=[
            jax.ShapeDtypeStruct((rows, width), BF16),
            jax.ShapeDtypeStruct((rows, width), BF16),
            jax.ShapeDtypeStruct((8, rows), F32),
        ],
        name="finish",
    )(tokens, gain, *parts)


def peak_kernel(blocks, words, places_ref, *refs):
    block_refs = refs[:blocks]
    head_ref, out_ref, table, best, sems = refs[blocks:]
    rows = block_refs[0].shape[0]
    step = pl.program_id(0)
    tile = head_ref.shape[1]

    @pl.when(step == 0)
    def _():
        copies = [
            pltpu.make_async_copy(ref, table.at[pl.ds(i * rows, rows)], sems.at[i])
            for i, ref in enumerate(block_refs)
        ]
        for c in copies:
            c.start()
        for c in copies:
            c.wait()
        best[...] = jnp.full(best.shape, -jnp.inf, F32)

    logits = jnp.dot(table[...], head_ref[...], preferred_element_type=F32)
    word = lax.broadcasted_iota(jnp.int32, logits.shape, 1) + step * tile
    best[...] = jnp.maximum(best[...], jnp.where(word < words, logits, -jnp.inf))

    @pl.when(step == pl.num_programs(0) - 1)
    def _():
        peak = jnp.max(best[...], axis=1, keepdims=True)
        line = jnp.transpose(jnp.broadcast_to(peak, (peak.shape[0], 128)))[0:1, :]
        target = lax.broadcasted_iota(jnp.int32, out_ref.shape, 0)
        out = jnp.full(out_ref.shape, -jnp.inf, F32)
        for i in range(blocks):
            out = jnp.where(target == places_ref[i], line[:, i * rows : (i + 1) * rows], out)
        out_ref[...] = out


def peaks(places, block_list, head_weight, n_exp):
    blocks = len(block_list)
    rows, width = block_list[0].shape
    words = head_weight.shape[1]
    tile = 512
    steps = pl.cdiv(words, tile)
    return pl.pallas_call(
        functools.partial(peak_kernel, blocks, words),
        grid=(steps,),
        in_specs=[pl.BlockSpec(memory_space=pltpu.SMEM)]
        + [pl.BlockSpec(memory_space=pl.ANY)] * blocks
        + [pl.BlockSpec((width, tile), lambda i: (0, i))],
        out_specs=pl.BlockSpec((n_exp, rows), lambda i: (0, 0)),
        out_shape=jax.ShapeDtypeStruct((n_exp, rows), F32),
        scratch_shapes=[
            pltpu.VMEM((blocks * rows, width), BF16),
            pltpu.VMEM((blocks * rows, tile), F32),
            pltpu.SemaphoreType.DMA((blocks,)),
        ],
        compiler_params=pltpu.CompilerParams(
            vmem_limit_bytes=VMEM_LIMIT, dimension_semantics=("arbitrary",)
        ),
        cost_estimate=pl.CostEstimate(
            flops=2 * blocks * rows * width * words,
            bytes_accessed=2 * width * words + 2 * blocks * rows * width,
            transcendentals=0,
        ),
        name="peaks",
    )(places, *block_list, head_weight)


def add(a, b):
    return (a.astype(F32) + b.astype(F32)).astype(BF16)


def per_device(
    n_req,
    n_exp,
    tokens,
    routes,
    router,
    gate_weight,
    up_weight,
    down_weight,
    norm_gain,
    head_weight,
    lengths,
):
    row_count, width = tokens.shape
    experts = router.shape[1]
    half_exp = n_exp // 2
    group_size = n_req * n_exp // (2 * experts)
    r = lax.axis_index("req")
    e = lax.axis_index("exp")
    expert = ((r * half_exp + e % half_exp) // group_size).astype(jnp.int32).reshape(1)

    def send(x, flips0, flips1=None):
        pairs = flip_pairs(n_req, n_exp, (flips0, flips0 if flips1 is None else flips1))
        return lax.ppermute(x, AXES, pairs)

    core = [("req", 1)]
    dims = [("req", b) for b in bits_below(n_req, 2)] + [("exp", b) for b in bits_below(half_exp)]
    extra, dims = dims[3:], dims[:3]
    turned = dims[1:] + dims[:1]

    def hop(x, *js):
        return send(x, [dims[j] for j in js], [turned[j] for j in js])

    block = prepare(tokens, routes, router)
    for d in extra:
        block = jnp.concatenate([block, send(block, [d])], axis=0)
    near = [block]
    near += [hop(b, 0) for b in near]
    near += [hop(b, 1) for b in near]
    far = [hop(b, 2) for b in near]
    near += [send(b, core) for b in near]
    far += [send(b, core) for b in far]
    cap = CAP * block.shape[0] // row_count
    weights = (gate_weight, up_weight, down_weight)

    *near_out, near_other = run_expert(expert, near, *weights, cap)
    *far_out, far_other = run_expert(expert, far, *weights, cap)
    rows = block.shape[0]

    def with_core(own, other):
        got = send(other, core)
        return [add(b, got[i * rows : (i + 1) * rows]) for i, b in enumerate(own)]

    near_sum = with_core(near_out, near_other)
    n3 = hop(near_sum[3], 1)
    n2 = hop(near_sum[2], 1)
    n1 = hop(add(near_sum[1], n3), 0)
    far_sum = with_core(far_out, far_other)
    f3 = hop(far_sum[3], 1)
    f2 = hop(far_sum[2], 1)
    f1 = hop(add(far_sum[1], f3), 0, 2)
    f0 = hop(add(far_sum[0], f2), 2)
    parts = [near_sum[0], n2, n1, f0, f1]
    for d in reversed(extra):
        merged = sum(p.astype(F32) for p in parts).astype(BF16)
        size = merged.shape[0] // 2
        parts = [merged[:size], send(merged[size:], [d])]
    hidden_out, normed, square = finish(tokens, norm_gain.reshape(1, width), parts)

    near_dims = [("exp", b) for b in bits_below(half_exp)]
    near_turn = near_dims[1:] + near_dims[:1]
    across = [("exp", half_exp)]

    def spread(first):
        held, moved = [first], [(0, 0)]
        for a, b in zip(near_dims, near_turn):
            held += [send(x, [a], [b]) for x in held]
            moved += [(p ^ a[1], q ^ b[1]) for p, q in moved]
        return held, moved

    far_first = send(normed, across)
    near_blocks, moved = spread(normed)
    far_blocks, _ = spread(far_first)
    is_second = r % 2 == 1
    places = jnp.stack([jnp.where(is_second, e ^ q, e ^ p) for p, q in moved]).astype(jnp.int32)
    near_peak = peaks(places, near_blocks, head_weight, n_exp)
    far_peak = peaks(places ^ half_exp, far_blocks, head_weight, n_exp)
    got = lax.all_to_all(jnp.maximum(near_peak, far_peak), "exp", 0, 0, tiled=True)
    row_max = jnp.max(got, axis=0)

    request_ends = jnp.cumsum(lengths[0])
    position = jnp.arange(row_count, dtype=jnp.int32)
    request_of = jnp.sum((position[:, None] >= request_ends[None, :]).astype(jnp.int32), axis=1)
    member = request_of[:, None] == jnp.arange(lengths.shape[1], dtype=jnp.int32)[None, :]
    request_sq = jnp.sum(jnp.where(member, square[0][:, None], F32(0.0)), axis=0)
    request_norm = jnp.sqrt(request_sq / (lengths[0].astype(F32) * width))
    request_max = jnp.max(jnp.where(member, row_max[:, None], F32(-jnp.inf)), axis=0)
    return (hidden_out, request_norm, request_max)


def solution(mesh):
    placed = (
        P(AXES, None),
        P(AXES, None),
        P(),
        P(None, AXES),
        P(None, AXES),
        P(AXES, None),
        P(),
        P(None, "exp"),
        P(AXES, None),
    )
    return jax.shard_map(
        functools.partial(per_device, mesh.shape["req"], mesh.shape["exp"]),
        mesh=mesh,
        in_specs=placed,
        out_specs=(P(AXES, None), P(AXES), P(AXES)),
        check_vma=False,
    )
```

```python
import functools

import jax
import jax.numpy as jnp
from jax import lax
from jax.experimental import pallas as pl
from jax.experimental.pallas import tpu as pltpu
from jax.sharding import PartitionSpec as P

CAP = 24
META = 128
CUT = 768
HAND_ON = 0
VMEM_LIMIT = 60 * 1024 * 1024

norm_eps = 1e-05
AXES = ("req", "exp")
F32 = jnp.float32
BF16 = jnp.bfloat16


def flip_pairs(n_req, n_exp, dim_of_core):
    pairs = []
    for r in range(n_req):
        for e in range(n_exp):
            flips = dim_of_core[r & 1]
            pr, pe = r, e
            for axis, bit in flips:
                if axis == "req":
                    pr ^= bit
                else:
                    pe ^= bit
            pairs.append((r * n_exp + e, pr * n_exp + pe))
    return pairs


def bits_below(n, first=1):
    out = []
    b = first
    while b < n:
        out.append(b)
        b *= 2
    return out


def prepare_kernel(tokens_ref, routes_ref, router_ref, out_ref):
    width = tokens_ref.shape[1]
    rows = tokens_ref.shape[0]
    t = tokens_ref[...]
    out_ref[:, :width] = t
    logits = lax.dot_general(
        t, router_ref[...], (((1,), (1,)), ((), ())), preferred_element_type=F32
    )
    gating = 1.0 / (1.0 + jnp.exp(-logits))
    routes = jnp.transpose(
        jnp.concatenate([routes_ref[...].astype(F32), jnp.zeros((6, rows), F32)], axis=0)
    )
    lane = lax.broadcasted_iota(jnp.int32, (rows, META), 1)
    expert = lax.broadcasted_iota(jnp.int32, gating.shape, 1).astype(F32)
    meta = jnp.zeros((rows, META), F32)
    for k in range(2):
        ids = routes[:, k : k + 1]
        chosen = jnp.sum(jnp.where(expert == ids, gating, 0.0), axis=1, keepdims=True)
        high = chosen.astype(BF16).astype(F32)
        mid = (chosen - high).astype(BF16).astype(F32)
        low = chosen - high - mid
        for j, piece in enumerate((ids, high, mid, low)):
            meta = jnp.where(lane == 4 * k + j, piece, meta)
    out_ref[:, width:] = meta.astype(BF16)


def prepare(tokens, routes, router):
    rows, width = tokens.shape
    return pl.pallas_call(
        prepare_kernel,
        out_shape=jax.ShapeDtypeStruct((rows, width + META), BF16),
        compiler_params=params(8 * 1024 * 1024),
        name="prepare",
    )(tokens, routes.T, router.T)


def near_core(x):
    return pltpu.with_memory_space_constraint(x, pltpu.VMEM)


LOCAL = pl.BlockSpec(memory_space=pltpu.VMEM)


def params(limit):
    return pltpu.CompilerParams(vmem_limit_bytes=limit)


def fetch_kernel(parts, from_ref, after_ref, to_ref, sems):
    rows = to_ref.shape[0] // parts
    copies = [
        pltpu.make_async_copy(
            from_ref.at[pl.ds(i * rows, rows)], to_ref.at[pl.ds(i * rows, rows)], sems.at[i]
        )
        for i in range(parts)
    ]
    for c in copies:
        c.start()
    for c in copies:
        c.wait()


def fetch(x, after):
    parts = max(p for p in range(1, 9) if x.shape[0] % (16 * p) == 0)
    size = x.size * x.dtype.itemsize
    return pl.pallas_call(
        functools.partial(fetch_kernel, parts),
        in_specs=[pl.BlockSpec(memory_space=pl.ANY)] * 2,
        out_specs=LOCAL,
        out_shape=pltpu.VMEM(x.shape, x.dtype),
        scratch_shapes=[pltpu.SemaphoreType.DMA((parts,))],
        compiler_params=params(1024 * 1024),
        cost_estimate=pl.CostEstimate(flops=0, bytes_accessed=size, transcendentals=0),
        name="fetch",
    )(pltpu.with_memory_space_constraint(x, pltpu.HBM), after)


def pieces(size, want):
    return size // want if size % want == 0 else 1


def spans(size, want):
    return [(at, min(want, size - at)) for at in range(0, size, want)]


def expert_kernel(blocks, slots, held, hand_on, expert_ref, *refs):
    half = blocks // 2
    block_refs, refs = refs[:blocks], refs[blocks:]
    weight_refs, refs = refs[:3], refs[3:]
    own_refs, other_ref, refs = refs[:half], refs[half], refs[half + 1 :]
    kept, refs = refs[:hand_on], refs[hand_on:]
    table, hidden, weighted, refs = refs[0], refs[1], refs[2], refs[3:]
    loaded, sems = list(kept) + list(refs[:-1]), refs[-1]
    rows = block_refs[0].shape[0]
    width, units = weight_refs[0].shape
    count = blocks * rows
    weights = list(weight_refs[:held]) + loaded
    cuts = [spans(units, CUT), spans(units, CUT), spans(width, CUT)]
    waits = [[] for _ in range(3)]

    def load(w, j):
        if w >= held:
            at, size = cuts[w][j]
            c = pltpu.make_async_copy(
                weight_refs[w].at[:, pl.ds(at, size)],
                weights[w].at[:, pl.ds(at, size)],
                sems.at[w, j],
            )
            c.start()
            waits[w].append(c)

    def arrive(w, j):
        if w >= held:
            waits[w][j].wait()

    for j in range(len(cuts[0])):
        load(0, j)
        load(1, j)
    for j in range(len(cuts[2])):
        load(2, j)
    for i, ref in enumerate(block_refs):
        table[i * rows : (i + 1) * rows, :] = ref[...]
    own = expert_ref[0].astype(F32)
    meta = jnp.transpose(table[:, width:].astype(F32))
    first = meta[0:1] == own
    second = meta[4:5] == own
    member = jnp.logical_or(first, second)
    weight = jnp.where(first, meta[1:2] + meta[2:3] + meta[3:4], meta[5:6] + meta[6:7] + meta[7:8])
    flag = jnp.where(member, 1.0, 0.0)
    part = min(count, 512)
    before = lax.broadcasted_iota(jnp.int32, (part, part), 0) < lax.broadcasted_iota(
        jnp.int32, (part, part), 1
    )
    before = jnp.where(before, 1.0, 0.0).astype(BF16)
    ranks, base = [], jnp.zeros((1, 1), F32)
    for at in range(0, count, part):
        some = flag[:, at : at + part]
        rank = jnp.dot(
            jnp.broadcast_to(some, (8, part)).astype(BF16), before, preferred_element_type=F32
        )
        ranks.append(rank[0:1] + base)
        base = base + jnp.sum(some, axis=1, keepdims=True)
    rank = jnp.where(member, jnp.concatenate(ranks, axis=1), -1.0).astype(jnp.int32)
    chosen = lax.broadcasted_iota(jnp.int32, (slots, count), 0) == rank
    place = jnp.where(chosen, 1.0, 0.0).astype(BF16)
    scale = jnp.sum(jnp.where(chosen, weight, 0.0), axis=1, keepdims=True)
    x = jnp.dot(place, table[:, :width], preferred_element_type=F32).astype(BF16)
    back = jnp.transpose(place)
    for j, (start, size) in enumerate(cuts[0]):
        arrive(0, j)
        arrive(1, j)
        for at, some in spans(size, 256):
            at = slice(start + at, start + at + some)
            g = jnp.dot(x, weights[0][:, at], preferred_element_type=F32)
            u = jnp.dot(x, weights[1][:, at], preferred_element_type=F32)
            hidden[:, at] = (g / (1.0 + jnp.exp(-g)) * u).astype(BF16)
    for j, (start, size) in enumerate(cuts[2]):
        arrive(2, j)
        for at, some in spans(size, 256):
            at = slice(start + at, start + at + some)
            y = jnp.dot(hidden[...], weights[2][:, at], preferred_element_type=F32)
            weighted[:, at] = (y * scale).astype(BF16)
    for start, size in spans(width, 1024):
        at = slice(start, start + size)
        spread = jnp.dot(back, weighted[:, at], preferred_element_type=F32).astype(BF16)
        for i, ref in enumerate(own_refs):
            ref[:, at] = spread[i * rows : (i + 1) * rows]
        other_ref[:, at] = spread[half * rows :]


def run_expert(expert, block_list, weights, cap, held, hand_on):
    blocks = len(block_list)
    rows = block_list[0].shape[0]
    width, units = weights[0].shape
    slots = blocks * cap
    count = blocks * rows
    half = blocks // 2
    loads = [pltpu.VMEM(w.shape, BF16) for w in weights]
    cuts = len(spans(max(units, width), CUT))
    scoped = sum(2 * width * units for _ in weights[max(held, hand_on) :])
    return pl.pallas_call(
        functools.partial(expert_kernel, blocks, slots, held, hand_on),
        in_specs=[pl.BlockSpec(memory_space=pltpu.SMEM)]
        + [LOCAL] * (blocks + held)
        + [pl.BlockSpec(memory_space=pl.ANY)] * (3 - held),
        out_specs=[LOCAL] * (half + 1 + hand_on),
        out_shape=[jax.ShapeDtypeStruct((rows, width), BF16)] * half
        + [jax.ShapeDtypeStruct((half * rows, width), BF16)]
        + loads[:hand_on],
        scratch_shapes=[
            pltpu.VMEM((count, width + META), BF16),
            pltpu.VMEM((slots, units), BF16),
            pltpu.VMEM((slots, width), BF16),
            *loads[max(held, hand_on) :],
            pltpu.SemaphoreType.DMA((3, cuts)),
        ],
        compiler_params=params(scoped + 10 * count * (width + META)),
        cost_estimate=pl.CostEstimate(
            flops=10 * slots * width * units + 4 * slots * count * width,
            bytes_accessed=6 * width * units,
            transcendentals=slots * units,
        ),
        name="expert",
    )(
        expert,
        *map(near_core, block_list),
        *map(near_core, weights[:held]),
        *(pltpu.with_memory_space_constraint(w, pltpu.HBM) for w in weights[held:]),
    )


def add_kernel(count, rows, *refs):
    own, other, out = refs[:count], refs[count:-count], refs[-count:]
    for i in range(count):
        got = other[0][i * rows : (i + 1) * rows] if len(other) == 1 else other[i][...]
        out[i][...] = (own[i][...].astype(F32) + got.astype(F32)).astype(BF16)


def add_blocks(own, other):
    count = len(own)
    rows, width = own[0].shape
    return pl.pallas_call(
        functools.partial(add_kernel, count, rows),
        in_specs=[LOCAL] * (count + len(other)),
        out_specs=[LOCAL] * count,
        out_shape=[jax.ShapeDtypeStruct((rows, width), BF16)] * count,
        compiler_params=params(12 * count * rows * width),
        cost_estimate=pl.CostEstimate(
            flops=count * rows * width, bytes_accessed=6 * count * rows * width, transcendentals=0
        ),
        name="add_blocks",
    )(*own, *other)


def finish_kernel(parts, lengths_ref, tokens_ref, gain_ref, *refs):
    hidden_ref, normed_ref, norm_ref = refs[parts:]
    total = refs[0][...].astype(F32)
    for ref in refs[1:parts]:
        total = total + ref[...].astype(F32)
    hidden = (tokens_ref[...].astype(F32) + total).astype(BF16)
    hidden_ref[...] = hidden
    wide = hidden.astype(F32)
    width = wide.shape[1]
    square = jnp.sum(wide * wide, axis=1, keepdims=True)
    normed_ref[...] = (wide * lax.rsqrt(square / width + norm_eps) * gain_ref[...]).astype(BF16)
    row = lax.broadcasted_iota(jnp.int32, square.shape, 0)
    lane = lax.broadcasted_iota(jnp.int32, norm_ref.shape, 1)
    out, start = jnp.zeros(norm_ref.shape, F32), 0
    for j in range(norm_ref.shape[1]):
        end = start + lengths_ref[0, j]
        member = jnp.logical_and(row >= start, row < end)
        mean = jnp.sum(jnp.where(member, square, 0.0), axis=0, keepdims=True) / (
            lengths_ref[0, j].astype(F32) * width
        )
        out = jnp.where(lane == j, jnp.sqrt(mean), out)
        start = end
    norm_ref[...] = out


def finish(lengths, tokens, gain, parts):
    rows, width = tokens.shape
    return pl.pallas_call(
        functools.partial(finish_kernel, len(parts)),
        in_specs=[pl.BlockSpec(memory_space=pltpu.SMEM)] + [LOCAL] * (2 + len(parts)),
        out_specs=[LOCAL] * 3,
        out_shape=[
            jax.ShapeDtypeStruct((rows, width), BF16),
            jax.ShapeDtypeStruct((rows, width), BF16),
            jax.ShapeDtypeStruct(lengths.shape, F32),
        ],
        compiler_params=params(8 * 1024 * 1024),
        name="finish",
    )(lengths, tokens, gain, *parts)


def request_kernel(lengths_ref, *refs):
    out_ref = refs[-1]
    peak = refs[0][...]
    for ref in refs[1:-1]:
        peak = jnp.maximum(peak, ref[...])
    row = lax.broadcasted_iota(jnp.int32, peak.shape, 1)
    lane = lax.broadcasted_iota(jnp.int32, out_ref.shape, 1)
    out, start = jnp.zeros(out_ref.shape, F32), 0
    for j in range(out_ref.shape[1]):
        end = start + lengths_ref[0, j]
        member = jnp.logical_and(row >= start, row < end)
        best = jnp.max(jnp.where(member, peak, -jnp.inf), axis=1, keepdims=True)
        out = jnp.where(lane == j, best, out)
        start = end
    out_ref[...] = out


def request_peaks(lengths, found):
    return pl.pallas_call(
        request_kernel,
        in_specs=[pl.BlockSpec(memory_space=pltpu.SMEM)] + [LOCAL] * len(found),
        out_specs=LOCAL,
        out_shape=jax.ShapeDtypeStruct(lengths.shape, F32),
        compiler_params=params(1024 * 1024),
        name="request_peaks",
    )(lengths, *found)


def peak_kernel(blocks, *refs):
    block_refs = refs[:blocks]
    head_ref, out_ref, table = refs[blocks:]
    rows = block_refs[0].shape[0]
    words = head_ref.shape[0]
    for i, ref in enumerate(block_refs):
        table[i * rows : (i + 1) * rows, :] = ref[...]
    tile = max(t for t in range(16, 513, 16) if words % t == 0)
    best = None
    for j in range(words // tile):
        logits = lax.dot_general(
            head_ref[j * tile : (j + 1) * tile, :],
            table[...],
            (((1,), (1,)), ((), ())),
            preferred_element_type=F32,
        )
        peak = jnp.max(logits, axis=0, keepdims=True)
        best = peak if best is None else jnp.maximum(best, peak)
    for i in range(blocks):
        out_ref[i : i + 1, :] = best[:, i * rows : (i + 1) * rows]


def peaks(block_list, words_first):
    blocks = len(block_list)
    rows, width = block_list[0].shape
    words = words_first.shape[0]
    return pl.pallas_call(
        functools.partial(peak_kernel, blocks),
        in_specs=[LOCAL] * (blocks + 1),
        out_specs=LOCAL,
        out_shape=jax.ShapeDtypeStruct((blocks, rows), F32),
        scratch_shapes=[pltpu.VMEM((blocks * rows, width), BF16)],
        compiler_params=params(12 * 1024 * 1024),
        cost_estimate=pl.CostEstimate(
            flops=2 * blocks * rows * width * words,
            bytes_accessed=2 * blocks * rows * width,
            transcendentals=0,
        ),
        name="peaks",
    )(*map(near_core, block_list), near_core(words_first))


def per_device(
    n_req,
    n_exp,
    tokens,
    routes,
    router,
    gate_weight,
    up_weight,
    down_weight,
    norm_gain,
    head_weight,
    lengths,
):
    row_count, width = tokens.shape
    experts = router.shape[1]
    half_exp = n_exp // 2
    group_size = n_req * n_exp // (2 * experts)
    r = lax.axis_index("req")
    e = lax.axis_index("exp")
    expert = ((r * half_exp + e % half_exp) // group_size).astype(jnp.int32).reshape(1)

    def send(x, flips0, flips1=None):
        pairs = flip_pairs(n_req, n_exp, (flips0, flips0 if flips1 is None else flips1))
        return lax.ppermute(x, AXES, pairs)

    core = [("req", 1)]
    dims = [("req", b) for b in bits_below(n_req, 2)] + [("exp", b) for b in bits_below(half_exp)]
    extra, dims = dims[3:], dims[:3]
    turned = dims[1:] + dims[:1]

    def hop(x, *js):
        return send(x, [dims[j] for j in js], [turned[j] for j in js])

    block = prepare(tokens, routes, router)
    for d in extra:
        block = jnp.concatenate([block, send(block, [d])], axis=0)
    near = [block, hop(block, 0)]
    near += [hop(b, 1) for b in near]
    far = [hop(b, 2) for b in near]
    near += [send(b, core) for b in near]
    cap = CAP * block.shape[0] // row_count
    rows = block.shape[0]
    blocks = len(near)

    weights = [gate_weight, up_weight, down_weight]
    out = run_expert(expert, near, weights, cap, 0, HAND_ON)
    half = blocks // 2
    near_out, near_other, weights[:HAND_ON] = out[:half], out[half], out[half + 1 :]
    far, near_out = lax.optimization_barrier((far, near_out))
    far += [send(b, core) for b in far]
    out = run_expert(expert, far, weights, cap, HAND_ON, 0)
    far_out, far_other = out[:half], out[half]
    near_sum = add_blocks(near_out, [send(near_other, core)])
    n3 = hop(near_sum[3], 1)
    n2 = hop(near_sum[2], 1)
    n1 = hop(add_blocks([near_sum[1]], [n3])[0], 0)
    words_first = fetch(head_weight.T, far_other)
    far_sum = add_blocks(far_out, [send(far_other, core)])
    f3 = hop(far_sum[3], 1)
    f2 = hop(far_sum[2], 1)
    f1 = hop(add_blocks([far_sum[1]], [f3])[0], 0, 2)
    f0 = hop(add_blocks([far_sum[0]], [f2])[0], 2)
    parts = [near_sum[0], n2, n1, f0, f1]
    for d in reversed(extra):
        merged = sum(p.astype(F32) for p in parts).astype(BF16)
        size = merged.shape[0] // 2
        parts = [merged[:size], send(merged[size:], [d])]
    parts, words_first = lax.optimization_barrier((parts, words_first))
    hidden_out, normed, request_norm = finish(lengths, tokens, norm_gain.reshape(1, width), parts)

    near_dims = [("exp", b) for b in bits_below(half_exp)]
    near_turn = near_dims[1:] + near_dims[:1]
    across = ("exp", half_exp)
    ways = [([], [])]
    for p, q in zip(near_dims, near_turn):
        ways += [(a + [p], b + [q]) for a, b in ways]
    far_first = send(normed, [across])
    near_blocks = [normed] + [send(normed, *w) for w in ways[1:]]
    far_blocks = [far_first] + [send(far_first, *w) for w in ways[1:]]
    near_blocks, far_first = lax.optimization_barrier((near_blocks, far_first))
    near_peak = peaks(near_blocks, words_first)
    far_first, near_peak = lax.optimization_barrier((far_first, near_peak))
    first_peak = peaks([far_first], words_first)
    far_peak = peaks(far_blocks[1:], words_first)
    found = [near_peak[0:1]]
    found += [send(near_peak[i : i + 1], *w) for i, w in enumerate(ways) if i > 0]
    found += [send(first_peak, [across])]
    found += [
        send(far_peak[i : i + 1], p + [across], q + [across])
        for i, (p, q) in enumerate(ways[1:])
    ]
    request_max = request_peaks(lengths, found)
    return (hidden_out, request_norm[0], request_max[0])


def solution(mesh):
    placed = (
        P(AXES, None),
        P(AXES, None),
        P(),
        P(None, AXES),
        P(None, AXES),
        P(AXES, None),
        P(),
        P(None, "exp"),
        P(AXES, None),
    )
    return jax.shard_map(
        functools.partial(per_device, mesh.shape["req"], mesh.shape["exp"]),
        mesh=mesh,
        in_specs=placed,
        out_specs=(P(AXES, None), P(AXES), P(AXES)),
        check_vma=False,
    )
```

```python
import functools

import jax
import jax.numpy as jnp
from jax import lax
from jax.experimental import pallas as pl
from jax.experimental.pallas import tpu as pltpu
from jax.sharding import PartitionSpec as P

CAP = 24
META = 128
CUT = 768
DOWN_CUT = 512
SPREAD = 1024
VMEM_LIMIT = 60 * 1024 * 1024

norm_eps = 1e-05
AXES = ("req", "exp")
F32 = jnp.float32
BF16 = jnp.bfloat16
SHORT = pl.CostEstimate(flops=1, bytes_accessed=1, transcendentals=0)


def flip_pairs(n_req, n_exp, dim_of_core):
    pairs = []
    for r in range(n_req):
        for e in range(n_exp):
            flips = dim_of_core[r & 1]
            pr, pe = r, e
            for axis, bit in flips:
                if axis == "req":
                    pr ^= bit
                else:
                    pe ^= bit
            pairs.append((r * n_exp + e, pr * n_exp + pe))
    return pairs


def bits_below(n, first=1):
    out = []
    b = first
    while b < n:
        out.append(b)
        b *= 2
    return out


def prepare_kernel(tokens_hbm, routes_hbm, router_hbm, out_ref, routes_ref, router_ref, sems):
    rows, width = tokens_hbm.shape
    copies = [
        pltpu.make_async_copy(tokens_hbm, out_ref.at[:, pl.ds(0, width)], sems.at[0]),
        pltpu.make_async_copy(router_hbm, router_ref, sems.at[1]),
        pltpu.make_async_copy(routes_hbm, routes_ref, sems.at[2]),
    ]
    for c in copies:
        c.start()
    for c in copies:
        c.wait()
    logits = lax.dot_general(
        out_ref[:, :width], router_ref[...], (((1,), (1,)), ((), ())), preferred_element_type=F32
    )
    gating = 1.0 / (1.0 + jnp.exp(-logits))
    routes = jnp.transpose(
        jnp.concatenate([routes_ref[...].astype(F32), jnp.zeros((6, rows), F32)], axis=0)
    )
    lane = lax.broadcasted_iota(jnp.int32, (rows, META), 1)
    expert = lax.broadcasted_iota(jnp.int32, gating.shape, 1).astype(F32)
    meta = jnp.zeros((rows, META), F32)
    for k in range(2):
        ids = routes[:, k : k + 1]
        chosen = jnp.sum(jnp.where(expert == ids, gating, 0.0), axis=1, keepdims=True)
        high = chosen.astype(BF16).astype(F32)
        mid = (chosen - high).astype(BF16).astype(F32)
        low = chosen - high - mid
        for j, piece in enumerate((ids, high, mid, low)):
            meta = jnp.where(lane == 4 * k + j, piece, meta)
    out_ref[:, width:] = meta.astype(BF16)


def in_hbm(x):
    return pltpu.with_memory_space_constraint(x, pltpu.HBM)


def prepare(tokens, routes, router):
    rows, width = tokens.shape
    return pl.pallas_call(
        prepare_kernel,
        in_specs=[pl.BlockSpec(memory_space=pl.ANY)] * 3,
        out_specs=pl.BlockSpec(memory_space=pltpu.VMEM),
        out_shape=jax.ShapeDtypeStruct((rows, width + META), BF16),
        scratch_shapes=[
            pltpu.VMEM(routes.shape[::-1], jnp.int32),
            pltpu.VMEM(router.shape[::-1], BF16),
            pltpu.SemaphoreType.DMA((3,)),
        ],
        compiler_params=params(8 * 1024 * 1024),
        name="prepare",
    )(in_hbm(tokens), in_hbm(routes.T), in_hbm(router.T))


def near_core(x):
    return pltpu.with_memory_space_constraint(x, pltpu.VMEM)


LOCAL = pl.BlockSpec(memory_space=pltpu.VMEM)


def params(limit):
    return pltpu.CompilerParams(vmem_limit_bytes=limit)


def fetch_kernel(parts, from_ref, after_ref, to_ref, sems):
    rows = to_ref.shape[0] // parts
    copies = [
        pltpu.make_async_copy(
            from_ref.at[pl.ds(i * rows, rows)], to_ref.at[pl.ds(i * rows, rows)], sems.at[i]
        )
        for i in range(parts)
    ]
    for c in copies:
        c.start()
    for c in copies:
        c.wait()


def fetch(x, after):
    parts = max(p for p in range(1, 9) if x.shape[0] % (16 * p) == 0)
    size = x.size * x.dtype.itemsize
    return pl.pallas_call(
        functools.partial(fetch_kernel, parts),
        in_specs=[pl.BlockSpec(memory_space=pl.ANY)] * 2,
        out_specs=LOCAL,
        out_shape=pltpu.VMEM(x.shape, x.dtype),
        scratch_shapes=[pltpu.SemaphoreType.DMA((parts,))],
        compiler_params=params(1024 * 1024),
        cost_estimate=SHORT,
        name="fetch",
    )(pltpu.with_memory_space_constraint(x, pltpu.HBM), after)


def spans(size, want):
    return [(at, min(want, size - at)) for at in range(0, size, want)]


def expert_kernel(blocks, slots, expert_ref, *refs):
    half = blocks // 2
    block_refs, refs = refs[:blocks], refs[blocks:]
    weight_refs, refs = refs[:3], refs[3:]
    own_refs, other_ref, refs = refs[:half], refs[half], refs[half + 1 :]
    table, hidden, weighted, *weights, sems = refs
    rows = block_refs[0].shape[0]
    width, units = weight_refs[0].shape
    count = blocks * rows
    cuts = [spans(units, CUT), spans(units, CUT), spans(width, DOWN_CUT)]
    waits = [[] for _ in range(3)]

    def load(w, j):
        at, size = cuts[w][j]
        c = pltpu.make_async_copy(
            weight_refs[w].at[:, pl.ds(at, size)],
            weights[w].at[:, pl.ds(at, size)],
            sems.at[w, j],
        )
        c.start()
        waits[w].append(c)

    for j in range(len(cuts[0])):
        load(0, j)
        load(1, j)
    for j in range(len(cuts[2])):
        load(2, j)
    for i, ref in enumerate(block_refs):
        table[i * rows : (i + 1) * rows, :] = ref[...]
    own = expert_ref[0].astype(F32)
    meta = jnp.transpose(table[:, width:].astype(F32))
    first = meta[0:1] == own
    second = meta[4:5] == own
    member = jnp.logical_or(first, second)
    weight = jnp.where(first, meta[1:2] + meta[2:3] + meta[3:4], meta[5:6] + meta[6:7] + meta[7:8])
    flag = jnp.where(member, 1.0, 0.0)
    part = min(count, 512)
    before = lax.broadcasted_iota(jnp.int32, (part, part), 0) < lax.broadcasted_iota(
        jnp.int32, (part, part), 1
    )
    before = jnp.where(before, 1.0, 0.0).astype(BF16)
    ranks, base = [], jnp.zeros((1, 1), F32)
    for at in range(0, count, part):
        some = flag[:, at : at + part]
        rank = jnp.dot(
            jnp.broadcast_to(some, (8, part)).astype(BF16), before, preferred_element_type=F32
        )
        ranks.append(rank[0:1] + base)
        base = base + jnp.sum(some, axis=1, keepdims=True)
    rank = jnp.where(member, jnp.concatenate(ranks, axis=1), -1.0).astype(jnp.int32)
    chosen = lax.broadcasted_iota(jnp.int32, (slots, count), 0) == rank
    place = jnp.where(chosen, 1.0, 0.0).astype(BF16)
    scale = jnp.sum(jnp.where(chosen, weight, 0.0), axis=1, keepdims=True)
    x = jnp.dot(place, table[:, :width], preferred_element_type=F32).astype(BF16)
    back = jnp.transpose(place)
    for j, (start, size) in enumerate(cuts[0]):
        waits[0][j].wait()
        waits[1][j].wait()
        for at, some in spans(size, 256):
            at = slice(start + at, start + at + some)
            g = jnp.dot(x, weights[0][:, at], preferred_element_type=F32)
            u = jnp.dot(x, weights[1][:, at], preferred_element_type=F32)
            hidden[:, at] = (g / (1.0 + jnp.exp(-g)) * u).astype(BF16)
    ready = 0
    for j, (start, size) in enumerate(cuts[2]):
        waits[2][j].wait()
        for at, some in spans(size, 256):
            at = slice(start + at, start + at + some)
            y = jnp.dot(hidden[...], weights[2][:, at], preferred_element_type=F32)
            weighted[:, at] = (y * scale).astype(BF16)
        end = start + size
        if end - ready < SPREAD and end < width:
            continue
        at = slice(ready, end)
        spread = jnp.dot(back, weighted[:, at], preferred_element_type=F32).astype(BF16)
        for i, ref in enumerate(own_refs):
            ref[:, at] = spread[i * rows : (i + 1) * rows]
        other_ref[:, at] = spread[half * rows :]
        ready = end


def run_expert(expert, block_list, weights, cap):
    blocks = len(block_list)
    rows = block_list[0].shape[0]
    width, units = weights[0].shape
    slots = blocks * cap
    count = blocks * rows
    half = blocks // 2
    cuts = max(len(spans(units, CUT)), len(spans(width, DOWN_CUT)))
    return pl.pallas_call(
        functools.partial(expert_kernel, blocks, slots),
        in_specs=[pl.BlockSpec(memory_space=pltpu.SMEM)]
        + [LOCAL] * blocks
        + [pl.BlockSpec(memory_space=pl.ANY)] * 3,
        out_specs=[LOCAL] * (half + 1),
        out_shape=[jax.ShapeDtypeStruct((rows, width), BF16)] * half
        + [jax.ShapeDtypeStruct((half * rows, width), BF16)],
        scratch_shapes=[
            pltpu.VMEM((count, width + META), BF16),
            pltpu.VMEM((slots, units), BF16),
            pltpu.VMEM((slots, width), BF16),
            *(pltpu.VMEM(w.shape, BF16) for w in weights),
            pltpu.SemaphoreType.DMA((3, cuts)),
        ],
        compiler_params=params(6 * width * units + 10 * count * (width + META)),
        cost_estimate=SHORT,
        name="expert",
    )(expert, *map(near_core, block_list), *map(in_hbm, weights))


def add_kernel(count, rows, *refs):
    own, other, out = refs[:count], refs[count:-count], refs[-count:]
    for i in range(count):
        got = other[0][i * rows : (i + 1) * rows] if len(other) == 1 else other[i][...]
        out[i][...] = (own[i][...].astype(F32) + got.astype(F32)).astype(BF16)


def add_blocks(own, other):
    count = len(own)
    rows, width = own[0].shape
    return pl.pallas_call(
        functools.partial(add_kernel, count, rows),
        in_specs=[LOCAL] * (count + len(other)),
        out_specs=[LOCAL] * count,
        out_shape=[jax.ShapeDtypeStruct((rows, width), BF16)] * count,
        compiler_params=params(12 * count * rows * width),
        cost_estimate=SHORT,
        name="add_blocks",
    )(*own, *other)


def finish_kernel(parts, lengths_ref, tokens_ref, gain_ref, *refs):
    hidden_ref, normed_ref, norm_ref = refs[parts:]
    total = refs[0][...].astype(F32)
    for ref in refs[1:parts]:
        total = total + ref[...].astype(F32)
    hidden = (tokens_ref[...].astype(F32) + total).astype(BF16)
    hidden_ref[...] = hidden
    wide = hidden.astype(F32)
    width = wide.shape[1]
    square = jnp.sum(wide * wide, axis=1, keepdims=True)
    normed_ref[...] = (wide * lax.rsqrt(square / width + norm_eps) * gain_ref[...]).astype(BF16)
    row = lax.broadcasted_iota(jnp.int32, square.shape, 0)
    lane = lax.broadcasted_iota(jnp.int32, norm_ref.shape, 1)
    out, start = jnp.zeros(norm_ref.shape, F32), 0
    for j in range(norm_ref.shape[1]):
        end = start + lengths_ref[0, j]
        member = jnp.logical_and(row >= start, row < end)
        mean = jnp.sum(jnp.where(member, square, 0.0), axis=0, keepdims=True) / (
            lengths_ref[0, j].astype(F32) * width
        )
        out = jnp.where(lane == j, jnp.sqrt(mean), out)
        start = end
    norm_ref[...] = out


def finish(lengths, tokens, gain, parts):
    rows, width = tokens.shape
    return pl.pallas_call(
        functools.partial(finish_kernel, len(parts)),
        in_specs=[pl.BlockSpec(memory_space=pltpu.SMEM)] + [LOCAL] * (2 + len(parts)),
        out_specs=[LOCAL] * 3,
        out_shape=[
            jax.ShapeDtypeStruct((rows, width), BF16),
            jax.ShapeDtypeStruct((rows, width), BF16),
            jax.ShapeDtypeStruct(lengths.shape, F32),
        ],
        compiler_params=params(8 * 1024 * 1024),
        name="finish",
    )(lengths, tokens, gain, *parts)


def request_kernel(lengths_ref, *refs):
    out_ref = refs[-1]
    peak = refs[0][...]
    for ref in refs[1:-1]:
        peak = jnp.maximum(peak, ref[...])
    row = lax.broadcasted_iota(jnp.int32, peak.shape, 1)
    lane = lax.broadcasted_iota(jnp.int32, out_ref.shape, 1)
    out, start = jnp.zeros(out_ref.shape, F32), 0
    for j in range(out_ref.shape[1]):
        end = start + lengths_ref[0, j]
        member = jnp.logical_and(row >= start, row < end)
        best = jnp.max(jnp.where(member, peak, -jnp.inf), axis=1, keepdims=True)
        out = jnp.where(lane == j, best, out)
        start = end
    out_ref[...] = out


def request_peaks(lengths, found):
    return pl.pallas_call(
        request_kernel,
        in_specs=[pl.BlockSpec(memory_space=pltpu.SMEM)] + [LOCAL] * len(found),
        out_specs=LOCAL,
        out_shape=jax.ShapeDtypeStruct(lengths.shape, F32),
        compiler_params=params(1024 * 1024),
        name="request_peaks",
    )(lengths, *found)


def peak_kernel(blocks, *refs):
    block_refs = refs[:blocks]
    head_ref, out_ref, table = refs[blocks:]
    rows = block_refs[0].shape[0]
    words = head_ref.shape[0]
    for i, ref in enumerate(block_refs):
        table[i * rows : (i + 1) * rows, :] = ref[...]
    tile = max(t for t in range(16, 513, 16) if words % t == 0)
    best = None
    for j in range(words // tile):
        logits = lax.dot_general(
            head_ref[j * tile : (j + 1) * tile, :],
            table[...],
            (((1,), (1,)), ((), ())),
            preferred_element_type=F32,
        )
        peak = jnp.max(logits, axis=0, keepdims=True)
        best = peak if best is None else jnp.maximum(best, peak)
    for i in range(blocks):
        out_ref[i : i + 1, :] = best[:, i * rows : (i + 1) * rows]


def peaks(block_list, words_first):
    blocks = len(block_list)
    rows, width = block_list[0].shape
    words = words_first.shape[0]
    return pl.pallas_call(
        functools.partial(peak_kernel, blocks),
        in_specs=[LOCAL] * (blocks + 1),
        out_specs=LOCAL,
        out_shape=jax.ShapeDtypeStruct((blocks, rows), F32),
        scratch_shapes=[pltpu.VMEM((blocks * rows, width), BF16)],
        compiler_params=params(12 * 1024 * 1024),
        cost_estimate=SHORT,
        name="peaks",
    )(*map(near_core, block_list), near_core(words_first))


def per_device(
    n_req,
    n_exp,
    tokens,
    routes,
    router,
    gate_weight,
    up_weight,
    down_weight,
    norm_gain,
    head_weight,
    lengths,
):
    row_count, width = tokens.shape
    experts = router.shape[1]
    half_exp = n_exp // 2
    group_size = n_req * n_exp // (2 * experts)
    r = lax.axis_index("req")
    e = lax.axis_index("exp")
    expert = ((r * half_exp + e % half_exp) // group_size).astype(jnp.int32).reshape(1)

    def send(x, flips0, flips1=None):
        pairs = flip_pairs(n_req, n_exp, (flips0, flips0 if flips1 is None else flips1))
        return lax.ppermute(x, AXES, pairs)

    core = [("req", 1)]
    dims = [("req", b) for b in bits_below(n_req, 2)] + [("exp", b) for b in bits_below(half_exp)]
    extra, dims = dims[3:], dims[:3]
    turned = dims[1:] + dims[:1]

    def hop(x, *js):
        return send(x, [dims[j] for j in js], [turned[j] for j in js])

    block = prepare(tokens, routes, router)
    for d in extra:
        block = jnp.concatenate([block, send(block, [d])], axis=0)
    near = [block, hop(block, 0)]
    near += [hop(b, 1) for b in near]
    far = [hop(b, 2) for b in near]
    near += [send(b, core) for b in near]
    cap = CAP * block.shape[0] // row_count
    rows = block.shape[0]

    weights = [gate_weight, up_weight, down_weight]
    *near_out, near_other = run_expert(expert, near, weights, cap)
    far, near_out = lax.optimization_barrier((far, near_out))
    far += [send(b, core) for b in far]
    *far_out, far_other = run_expert(expert, far, weights, cap)
    near_sum = add_blocks(near_out, [send(near_other, core)])
    n3 = hop(near_sum[3], 1)
    n2 = hop(near_sum[2], 1)
    n1 = hop(add_blocks([near_sum[1]], [n3])[0], 0)
    words_first = fetch(head_weight.T, far_other)
    far_sum = add_blocks(far_out, [send(far_other, core)])
    f3 = hop(far_sum[3], 1)
    f2 = hop(far_sum[2], 1)
    f1 = hop(add_blocks([far_sum[1]], [f3])[0], 0, 2)
    f0 = hop(add_blocks([far_sum[0]], [f2])[0], 2)
    parts = [near_sum[0], n2, n1, f0, f1]
    for d in reversed(extra):
        merged = sum(p.astype(F32) for p in parts).astype(BF16)
        size = merged.shape[0] // 2
        parts = [merged[:size], send(merged[size:], [d])]
    parts, words_first = lax.optimization_barrier((parts, words_first))
    hidden_out, normed, request_norm = finish(lengths, tokens, norm_gain.reshape(1, width), parts)

    exp_dims = [("exp", b) for b in bits_below(half_exp)]
    across = ("exp", half_exp)

    def tree(dims0, dims1):
        ways = [([], [])]
        for p, q in zip(dims0, dims1):
            ways += [(a + [p], b + [q]) for a, b in ways]
        return ways

    def peak_back(group):
        peak = peaks([held[k] for k in group], words_first)
        out = []
        for n, (side, i) in enumerate(group):
            p, q = trees[side][i]
            one = peak[n : n + 1]
            if side:
                one = send(one, p + [across], q + [across])
            elif p:
                one = send(one, p, q)
            out.append(one)
        return out, peak

    trees = tree(exp_dims[::-1], exp_dims[::-1]), tree(exp_dims, exp_dims[1:] + exp_dims[:1])
    singles = [i for i, (p, _) in enumerate(trees[0]) if len(p) == 1]
    first = send(normed, [across])
    first, *near_singles = lax.optimization_barrier(
        (first, *(send(normed, *trees[0][i]) for i in singles))
    )
    held = {(0, 0): normed, (1, 0): first}
    for i, x in zip(singles, near_singles):
        held[0, i] = x
        held[1, i] = send(first, *trees[1][i])
    early = sorted(k for k in held if k == (1, 0) or k[0] == 0)
    found, peak = peak_back(early)
    for i in singles:
        held[1, i], peak = lax.optimization_barrier((held[1, i], peak))
    for side in (1, 0):
        for i, (p, q) in enumerate(trees[side]):
            if len(p) > 1:
                before = trees[side].index((p[:-1], q[:-1]))
                held[side, i] = send(held[side, before], p[-1:], q[-1:])
    found += peak_back(sorted(k for k in held if k not in early))[0]
    request_max = request_peaks(lengths, found)
    return (hidden_out, request_norm[0], request_max[0])


def solution(mesh):
    placed = (
        P(AXES, None),
        P(AXES, None),
        P(),
        P(None, AXES),
        P(None, AXES),
        P(AXES, None),
        P(),
        P(None, "exp"),
        P(AXES, None),
    )
    return jax.shard_map(
        functools.partial(per_device, mesh.shape["req"], mesh.shape["exp"]),
        mesh=mesh,
        in_specs=placed,
        out_specs=(P(AXES, None), P(AXES), P(AXES)),
        check_vma=False,
    )
```

```python
import functools

import jax
import jax.numpy as jnp
from jax import lax
from jax.experimental import pallas as pl
from jax.experimental.pallas import tpu as pltpu
from jax.sharding import PartitionSpec as P

CAP = 24
META = 128
CUT = 512
DOWN_CUT = 512
SPREAD = 1024
VMEM_LIMIT = 60 * 1024 * 1024

norm_eps = 1e-05
AXES = ("req", "exp")
F32 = jnp.float32
BF16 = jnp.bfloat16
SHORT = pl.CostEstimate(flops=1, bytes_accessed=1, transcendentals=0)


def flip_pairs(n_req, n_exp, dim_of_core):
    pairs = []
    for r in range(n_req):
        for e in range(n_exp):
            flips = dim_of_core[r & 1]
            pr, pe = r, e
            for axis, bit in flips:
                if axis == "req":
                    pr ^= bit
                else:
                    pe ^= bit
            pairs.append((r * n_exp + e, pr * n_exp + pe))
    return pairs


def bits_below(n, first=1):
    out = []
    b = first
    while b < n:
        out.append(b)
        b *= 2
    return out


def prepare_kernel(tokens_hbm, routes_hbm, router_hbm, out_ref, routes_ref, router_ref, sems):
    rows, width = tokens_hbm.shape
    copies = [
        pltpu.make_async_copy(tokens_hbm, out_ref.at[:, pl.ds(0, width)], sems.at[0]),
        pltpu.make_async_copy(router_hbm, router_ref, sems.at[1]),
        pltpu.make_async_copy(routes_hbm, routes_ref, sems.at[2]),
    ]
    for c in copies:
        c.start()
    for c in copies:
        c.wait()
    logits = lax.dot_general(
        out_ref[:, :width], router_ref[...], (((1,), (1,)), ((), ())), preferred_element_type=F32
    )
    gating = 1.0 / (1.0 + jnp.exp(-logits))
    routes = jnp.transpose(
        jnp.concatenate([routes_ref[...].astype(F32), jnp.zeros((6, rows), F32)], axis=0)
    )
    lane = lax.broadcasted_iota(jnp.int32, (rows, META), 1)
    expert = lax.broadcasted_iota(jnp.int32, gating.shape, 1).astype(F32)
    meta = jnp.zeros((rows, META), F32)
    for k in range(2):
        ids = routes[:, k : k + 1]
        chosen = jnp.sum(jnp.where(expert == ids, gating, 0.0), axis=1, keepdims=True)
        high = chosen.astype(BF16).astype(F32)
        mid = (chosen - high).astype(BF16).astype(F32)
        low = chosen - high - mid
        for j, piece in enumerate((ids, high, mid, low)):
            meta = jnp.where(lane == 4 * k + j, piece, meta)
    out_ref[:, width:] = meta.astype(BF16)


def in_hbm(x):
    return pltpu.with_memory_space_constraint(x, pltpu.HBM)


def prepare(tokens, routes, router):
    rows, width = tokens.shape
    return pl.pallas_call(
        prepare_kernel,
        in_specs=[pl.BlockSpec(memory_space=pl.ANY)] * 3,
        out_specs=pl.BlockSpec(memory_space=pltpu.VMEM),
        out_shape=jax.ShapeDtypeStruct((rows, width + META), BF16),
        scratch_shapes=[
            pltpu.VMEM(routes.shape[::-1], jnp.int32),
            pltpu.VMEM(router.shape[::-1], BF16),
            pltpu.SemaphoreType.DMA((3,)),
        ],
        compiler_params=params(8 * 1024 * 1024),
        name="prepare",
    )(in_hbm(tokens), in_hbm(routes.T), in_hbm(router.T))


def near_core(x):
    return pltpu.with_memory_space_constraint(x, pltpu.VMEM)


LOCAL = pl.BlockSpec(memory_space=pltpu.VMEM)


def params(limit):
    return pltpu.CompilerParams(vmem_limit_bytes=limit)


def fetch_kernel(parts, from_ref, after_ref, to_ref, sems):
    rows = to_ref.shape[0] // parts
    copies = [
        pltpu.make_async_copy(
            from_ref.at[pl.ds(i * rows, rows)], to_ref.at[pl.ds(i * rows, rows)], sems.at[i]
        )
        for i in range(parts)
    ]
    for c in copies:
        c.start()
    for c in copies:
        c.wait()


def fetch(x, after):
    parts = max(p for p in range(1, 9) if x.shape[0] % (16 * p) == 0)
    size = x.size * x.dtype.itemsize
    return pl.pallas_call(
        functools.partial(fetch_kernel, parts),
        in_specs=[pl.BlockSpec(memory_space=pl.ANY)] * 2,
        out_specs=LOCAL,
        out_shape=pltpu.VMEM(x.shape, x.dtype),
        scratch_shapes=[pltpu.SemaphoreType.DMA((parts,))],
        compiler_params=params(1024 * 1024),
        cost_estimate=SHORT,
        name="fetch",
    )(pltpu.with_memory_space_constraint(x, pltpu.HBM), after)


def spans(size, want):
    return [(at, min(want, size - at)) for at in range(0, size, want)]


def expert_kernel(blocks, slots, expert_ref, *refs):
    half = blocks // 2
    block_refs, refs = refs[:blocks], refs[blocks:]
    weight_refs, refs = refs[:3], refs[3:]
    own_refs, other_ref, refs = refs[:half], refs[half], refs[half + 1 :]
    table, hidden, weighted, *weights, sems = refs
    rows = block_refs[0].shape[0]
    width, units = weight_refs[0].shape
    count = blocks * rows
    cuts = [spans(units, CUT), spans(units, CUT), spans(width, DOWN_CUT)]
    waits = [[] for _ in range(3)]

    def load(w, j):
        at, size = cuts[w][j]
        c = pltpu.make_async_copy(
            weight_refs[w].at[:, pl.ds(at, size)],
            weights[w].at[:, pl.ds(at, size)],
            sems.at[w, j],
        )
        c.start()
        waits[w].append(c)

    for j in range(len(cuts[0])):
        load(0, j)
        load(1, j)
    for j in range(len(cuts[2])):
        load(2, j)
    for i, ref in enumerate(block_refs):
        table[i * rows : (i + 1) * rows, :] = ref[...]
    own = expert_ref[0].astype(F32)
    meta = jnp.transpose(table[:, width:].astype(F32))
    first = meta[0:1] == own
    second = meta[4:5] == own
    member = jnp.logical_or(first, second)
    weight = jnp.where(first, meta[1:2] + meta[2:3] + meta[3:4], meta[5:6] + meta[6:7] + meta[7:8])
    flag = jnp.where(member, 1.0, 0.0)
    part = min(count, 512)
    before = lax.broadcasted_iota(jnp.int32, (part, part), 0) < lax.broadcasted_iota(
        jnp.int32, (part, part), 1
    )
    before = jnp.where(before, 1.0, 0.0).astype(BF16)
    ranks, base = [], jnp.zeros((1, 1), F32)
    for at in range(0, count, part):
        some = flag[:, at : at + part]
        rank = jnp.dot(
            jnp.broadcast_to(some, (8, part)).astype(BF16), before, preferred_element_type=F32
        )
        ranks.append(rank[0:1] + base)
        base = base + jnp.sum(some, axis=1, keepdims=True)
    rank = jnp.where(member, jnp.concatenate(ranks, axis=1), -1.0).astype(jnp.int32)
    chosen = lax.broadcasted_iota(jnp.int32, (slots, count), 0) == rank
    place = jnp.where(chosen, 1.0, 0.0).astype(BF16)
    scale = jnp.sum(jnp.where(chosen, weight, 0.0), axis=1, keepdims=True)
    x = jnp.dot(place, table[:, :width], preferred_element_type=F32).astype(BF16)
    back = jnp.transpose(place)
    for j, (start, size) in enumerate(cuts[0]):
        waits[0][j].wait()
        waits[1][j].wait()
        for at, some in spans(size, 256):
            at = slice(start + at, start + at + some)
            g = jnp.dot(x, weights[0][:, at], preferred_element_type=F32)
            u = jnp.dot(x, weights[1][:, at], preferred_element_type=F32)
            hidden[:, at] = (g / (1.0 + jnp.exp(-g)) * u).astype(BF16)
    ready = 0
    for j, (start, size) in enumerate(cuts[2]):
        waits[2][j].wait()
        for at, some in spans(size, 256):
            at = slice(start + at, start + at + some)
            y = jnp.dot(hidden[...], weights[2][:, at], preferred_element_type=F32)
            weighted[:, at] = (y * scale).astype(BF16)
        end = start + size
        if end - ready < SPREAD and end < width:
            continue
        at = slice(ready, end)
        spread = jnp.dot(back, weighted[:, at], preferred_element_type=F32).astype(BF16)
        for i, ref in enumerate(own_refs):
            ref[:, at] = spread[i * rows : (i + 1) * rows]
        other_ref[:, at] = spread[half * rows :]
        ready = end


def run_expert(expert, block_list, weights, cap):
    blocks = len(block_list)
    rows = block_list[0].shape[0]
    width, units = weights[0].shape
    slots = blocks * cap
    count = blocks * rows
    half = blocks // 2
    cuts = max(len(spans(units, CUT)), len(spans(width, DOWN_CUT)))
    return pl.pallas_call(
        functools.partial(expert_kernel, blocks, slots),
        in_specs=[pl.BlockSpec(memory_space=pltpu.SMEM)]
        + [LOCAL] * blocks
        + [pl.BlockSpec(memory_space=pl.ANY)] * 3,
        out_specs=[LOCAL] * (half + 1),
        out_shape=[jax.ShapeDtypeStruct((rows, width), BF16)] * half
        + [jax.ShapeDtypeStruct((half * rows, width), BF16)],
        scratch_shapes=[
            pltpu.VMEM((count, width + META), BF16),
            pltpu.VMEM((slots, units), BF16),
            pltpu.VMEM((slots, width), BF16),
            *(pltpu.VMEM(w.shape, BF16) for w in weights),
            pltpu.SemaphoreType.DMA((3, cuts)),
        ],
        compiler_params=params(6 * width * units + 10 * count * (width + META)),
        cost_estimate=SHORT,
        name="expert",
    )(expert, *map(near_core, block_list), *map(in_hbm, weights))


def add_kernel(count, rows, *refs):
    own, other, out = refs[:count], refs[count:-count], refs[-count:]
    for i in range(count):
        got = other[0][i * rows : (i + 1) * rows] if len(other) == 1 else other[i][...]
        out[i][...] = (own[i][...].astype(F32) + got.astype(F32)).astype(BF16)


def add_blocks(own, other):
    count = len(own)
    rows, width = own[0].shape
    return pl.pallas_call(
        functools.partial(add_kernel, count, rows),
        in_specs=[LOCAL] * (count + len(other)),
        out_specs=[LOCAL] * count,
        out_shape=[jax.ShapeDtypeStruct((rows, width), BF16)] * count,
        compiler_params=params(12 * count * rows * width),
        cost_estimate=SHORT,
        name="add_blocks",
    )(*own, *other)


def finish_kernel(parts, lengths_ref, tokens_ref, gain_ref, *refs):
    hidden_ref, normed_ref, norm_ref = refs[parts:]
    total = refs[0][...].astype(F32)
    for ref in refs[1:parts]:
        total = total + ref[...].astype(F32)
    hidden = (tokens_ref[...].astype(F32) + total).astype(BF16)
    hidden_ref[...] = hidden
    wide = hidden.astype(F32)
    width = wide.shape[1]
    square = jnp.sum(wide * wide, axis=1, keepdims=True)
    normed_ref[...] = (wide * lax.rsqrt(square / width + norm_eps) * gain_ref[...]).astype(BF16)
    row = lax.broadcasted_iota(jnp.int32, square.shape, 0)
    lane = lax.broadcasted_iota(jnp.int32, norm_ref.shape, 1)
    out, start = jnp.zeros(norm_ref.shape, F32), 0
    for j in range(norm_ref.shape[1]):
        end = start + lengths_ref[0, j]
        member = jnp.logical_and(row >= start, row < end)
        mean = jnp.sum(jnp.where(member, square, 0.0), axis=0, keepdims=True) / (
            lengths_ref[0, j].astype(F32) * width
        )
        out = jnp.where(lane == j, jnp.sqrt(mean), out)
        start = end
    norm_ref[...] = out


def finish(lengths, tokens, gain, parts):
    rows, width = tokens.shape
    return pl.pallas_call(
        functools.partial(finish_kernel, len(parts)),
        in_specs=[pl.BlockSpec(memory_space=pltpu.SMEM)] + [LOCAL] * (2 + len(parts)),
        out_specs=[LOCAL] * 3,
        out_shape=[
            jax.ShapeDtypeStruct((rows, width), BF16),
            jax.ShapeDtypeStruct((rows, width), BF16),
            jax.ShapeDtypeStruct(lengths.shape, F32),
        ],
        compiler_params=params(8 * 1024 * 1024),
        name="finish",
    )(lengths, tokens, gain, *parts)


def request_kernel(lengths_ref, *refs):
    out_ref = refs[-1]
    peak = refs[0][...]
    for ref in refs[1:-1]:
        peak = jnp.maximum(peak, ref[...])
    row = lax.broadcasted_iota(jnp.int32, peak.shape, 1)
    lane = lax.broadcasted_iota(jnp.int32, out_ref.shape, 1)
    out, start = jnp.zeros(out_ref.shape, F32), 0
    for j in range(out_ref.shape[1]):
        end = start + lengths_ref[0, j]
        member = jnp.logical_and(row >= start, row < end)
        best = jnp.max(jnp.where(member, peak, -jnp.inf), axis=1, keepdims=True)
        out = jnp.where(lane == j, best, out)
        start = end
    out_ref[...] = out


def request_peaks(lengths, found):
    return pl.pallas_call(
        request_kernel,
        in_specs=[pl.BlockSpec(memory_space=pltpu.SMEM)] + [LOCAL] * len(found),
        out_specs=LOCAL,
        out_shape=jax.ShapeDtypeStruct(lengths.shape, F32),
        compiler_params=params(1024 * 1024),
        name="request_peaks",
    )(lengths, *found)


def peak_kernel(blocks, start, stop, *refs):
    block_refs = refs[:blocks]
    head_ref, *prior, out_ref, table = refs[blocks:]
    rows = block_refs[0].shape[0]
    for i, ref in enumerate(block_refs):
        table[i * rows : (i + 1) * rows, :] = ref[...]
    words = stop - start
    tile = max(t for t in range(16, 513, 16) if words % t == 0)
    best = None
    for at in range(start, stop, tile):
        logits = lax.dot_general(
            head_ref[at : at + tile, :],
            table[...],
            (((1,), (1,)), ((), ())),
            preferred_element_type=F32,
        )
        peak = jnp.max(logits, axis=0, keepdims=True)
        best = peak if best is None else jnp.maximum(best, peak)
    for i in range(blocks):
        line = best[:, i * rows : (i + 1) * rows]
        if prior:
            line = jnp.maximum(line, prior[0][i : i + 1, :])
        out_ref[i : i + 1, :] = line


def peaks(block_list, words_first, start, stop, prior=()):
    blocks = len(block_list)
    rows, width = block_list[0].shape
    return pl.pallas_call(
        functools.partial(peak_kernel, blocks, start, stop),
        in_specs=[LOCAL] * (blocks + 1 + len(prior)),
        out_specs=LOCAL,
        out_shape=jax.ShapeDtypeStruct((blocks, rows), F32),
        scratch_shapes=[pltpu.VMEM((blocks * rows, width), BF16)],
        compiler_params=params(12 * 1024 * 1024),
        cost_estimate=SHORT,
        name="peaks",
    )(*map(near_core, block_list), near_core(words_first), *prior)


def per_device(
    n_req,
    n_exp,
    tokens,
    routes,
    router,
    gate_weight,
    up_weight,
    down_weight,
    norm_gain,
    head_weight,
    lengths,
):
    row_count, width = tokens.shape
    experts = router.shape[1]
    half_exp = n_exp // 2
    group_size = n_req * n_exp // (2 * experts)
    r = lax.axis_index("req")
    e = lax.axis_index("exp")
    expert = ((r * half_exp + e % half_exp) // group_size).astype(jnp.int32).reshape(1)

    def send(x, flips0, flips1=None):
        pairs = flip_pairs(n_req, n_exp, (flips0, flips0 if flips1 is None else flips1))
        return lax.ppermute(x, AXES, pairs)

    core = [("req", 1)]
    dims = [("req", b) for b in bits_below(n_req, 2)] + [("exp", b) for b in bits_below(half_exp)]
    extra, dims = dims[3:], dims[:3]
    turned = dims[1:] + dims[:1]

    def hop(x, *js):
        return send(x, [dims[j] for j in js], [turned[j] for j in js])

    block = prepare(tokens, routes, router)
    for d in extra:
        block = jnp.concatenate([block, send(block, [d])], axis=0)
    near = [block, hop(block, 0)]
    near += [hop(b, 1) for b in near]
    far = [hop(b, 2) for b in near]
    near += [send(b, core) for b in near]
    cap = CAP * block.shape[0] // row_count
    rows = block.shape[0]

    weights = [gate_weight, up_weight, down_weight]
    *near_out, near_other = run_expert(expert, near, weights, cap)
    far, near_out = lax.optimization_barrier((far, near_out))
    far += [send(b, core) for b in far]
    *far_out, far_other = run_expert(expert, far, weights, cap)
    near_sum = add_blocks(near_out, [send(near_other, core)])
    n3 = hop(near_sum[3], 1)
    n2 = hop(near_sum[2], 1)
    n1 = hop(add_blocks([near_sum[1]], [n3])[0], 0)
    words_first = fetch(head_weight.T, far_other)
    far_sum = add_blocks(far_out, [send(far_other, core)])
    f3 = hop(far_sum[3], 1)
    f2 = hop(far_sum[2], 1)
    f1 = hop(add_blocks([far_sum[1]], [f3])[0], 0, 2)
    f0 = hop(add_blocks([far_sum[0]], [f2])[0], 2)
    parts = [near_sum[0], n2, n1, f0, f1]
    for d in reversed(extra):
        merged = sum(p.astype(F32) for p in parts).astype(BF16)
        size = merged.shape[0] // 2
        parts = [merged[:size], send(merged[size:], [d])]
    parts, words_first = lax.optimization_barrier((parts, words_first))
    hidden_out, normed, request_norm = finish(lengths, tokens, norm_gain.reshape(1, width), parts)

    exp_dims = [("exp", b) for b in bits_below(half_exp)]
    across = ("exp", half_exp)

    def tree(dims0, dims1):
        ways = [([], [])]
        for p, q in zip(dims0, dims1):
            ways += [(a + [p], b + [q]) for a, b in ways]
        return ways

    def give_back(group, peak):
        out = []
        for n, (side, i) in enumerate(group):
            p, q = trees[side][i]
            one = peak[n : n + 1]
            if side:
                one = send(one, p + [across], q + [across])
            elif p:
                one = send(one, p, q)
            out.append(one)
        return out

    trees = tree(exp_dims[::-1], exp_dims[::-1]), tree(exp_dims[1:] + exp_dims[:1], exp_dims)
    singles = [i for i, (p, _) in enumerate(trees[0]) if len(p) == 1]
    first = send(normed, [across])
    first, *near_singles = lax.optimization_barrier(
        (first, *(send(normed, *trees[0][i]) for i in singles))
    )
    held = {(0, 0): normed, (1, 0): first}
    for i, x in zip(singles, near_singles):
        held[0, i] = x
        held[1, i] = send(first, *trees[1][i])
    early = sorted(k for k in held if k == (1, 0) or k[0] == 0)
    words = head_weight.shape[1]
    cut = words // 32 * 16
    early_in = [held[k] for k in early]
    peak = peaks(early_in, words_first, 0, cut)
    for i in singles:
        held[1, i], peak = lax.optimization_barrier((held[1, i], peak))
    for side in (0, 1):
        for i, (p, q) in enumerate(trees[side]):
            if len(p) > 1:
                before = trees[side].index((p[:-1], q[:-1]))
                held[side, i] = send(held[side, before], p[-1:], q[-1:])
    peak = peaks(early_in, words_first, cut, words, [peak])
    late = sorted((k for k in held if k not in early), reverse=True)
    found = give_back(early, peak)
    found += give_back(late, peaks([held[k] for k in late], words_first, 0, words))
    request_max = request_peaks(lengths, found)
    return (hidden_out, request_norm[0], request_max[0])


def solution(mesh):
    placed = (
        P(AXES, None),
        P(AXES, None),
        P(),
        P(None, AXES),
        P(None, AXES),
        P(AXES, None),
        P(),
        P(None, "exp"),
        P(AXES, None),
    )
    return jax.shard_map(
        functools.partial(per_device, mesh.shape["req"], mesh.shape["exp"]),
        mesh=mesh,
        in_specs=placed,
        out_specs=(P(AXES, None), P(AXES), P(AXES)),
        check_vma=False,
    )
```

```python
import functools

import jax
import jax.numpy as jnp
from jax import lax
from jax.experimental import pallas as pl
from jax.experimental.pallas import tpu as pltpu
from jax.sharding import PartitionSpec as P

CAP = 24
META = 128
CUT = 512
DOWN_CUT = 512
SPREAD = 1024
VMEM_LIMIT = 60 * 1024 * 1024

norm_eps = 1e-05
AXES = ("req", "exp")
F32 = jnp.float32
BF16 = jnp.bfloat16
SHORT = pl.CostEstimate(flops=1, bytes_accessed=1, transcendentals=0)


def flip_pairs(n_req, n_exp, dim_of_core):
    pairs = []
    for r in range(n_req):
        for e in range(n_exp):
            flips = dim_of_core[r & 1]
            pr, pe = r, e
            for axis, bit in flips:
                if axis == "req":
                    pr ^= bit
                else:
                    pe ^= bit
            pairs.append((r * n_exp + e, pr * n_exp + pe))
    return pairs


def bits_below(n, first=1):
    out = []
    b = first
    while b < n:
        out.append(b)
        b *= 2
    return out


def prepare_kernel(tokens_hbm, routes_hbm, router_hbm, out_ref, routes_ref, router_ref, sems):
    rows, width = tokens_hbm.shape
    copies = [
        pltpu.make_async_copy(tokens_hbm, out_ref.at[:, pl.ds(0, width)], sems.at[0]),
        pltpu.make_async_copy(router_hbm, router_ref, sems.at[1]),
        pltpu.make_async_copy(routes_hbm, routes_ref, sems.at[2]),
    ]
    for c in copies:
        c.start()
    for c in copies:
        c.wait()
    logits = lax.dot_general(
        out_ref[:, :width], router_ref[...], (((1,), (1,)), ((), ())), preferred_element_type=F32
    )
    gating = 1.0 / (1.0 + jnp.exp(-logits))
    routes = jnp.transpose(
        jnp.concatenate([routes_ref[...].astype(F32), jnp.zeros((6, rows), F32)], axis=0)
    )
    lane = lax.broadcasted_iota(jnp.int32, (rows, META), 1)
    expert = lax.broadcasted_iota(jnp.int32, gating.shape, 1).astype(F32)
    meta = jnp.zeros((rows, META), F32)
    for k in range(2):
        ids = routes[:, k : k + 1]
        chosen = jnp.sum(jnp.where(expert == ids, gating, 0.0), axis=1, keepdims=True)
        high = chosen.astype(BF16).astype(F32)
        mid = (chosen - high).astype(BF16).astype(F32)
        low = chosen - high - mid
        for j, piece in enumerate((ids, high, mid, low)):
            meta = jnp.where(lane == 4 * k + j, piece, meta)
    out_ref[:, width:] = meta.astype(BF16)


def in_hbm(x):
    return pltpu.with_memory_space_constraint(x, pltpu.HBM)


def prepare(tokens, routes, router):
    rows, width = tokens.shape
    return pl.pallas_call(
        prepare_kernel,
        in_specs=[pl.BlockSpec(memory_space=pl.ANY)] * 3,
        out_specs=pl.BlockSpec(memory_space=pltpu.VMEM),
        out_shape=jax.ShapeDtypeStruct((rows, width + META), BF16),
        scratch_shapes=[
            pltpu.VMEM(routes.shape[::-1], jnp.int32),
            pltpu.VMEM(router.shape[::-1], BF16),
            pltpu.SemaphoreType.DMA((3,)),
        ],
        compiler_params=params(8 * 1024 * 1024),
        name="prepare",
    )(in_hbm(tokens), in_hbm(routes.T), in_hbm(router.T))


def near_core(x):
    return pltpu.with_memory_space_constraint(x, pltpu.VMEM)


LOCAL = pl.BlockSpec(memory_space=pltpu.VMEM)


def params(limit):
    return pltpu.CompilerParams(vmem_limit_bytes=limit)


def fetch_kernel(parts, from_ref, after_ref, to_ref, sems):
    rows = to_ref.shape[0] // parts
    copies = [
        pltpu.make_async_copy(
            from_ref.at[pl.ds(i * rows, rows)], to_ref.at[pl.ds(i * rows, rows)], sems.at[i]
        )
        for i in range(parts)
    ]
    for c in copies:
        c.start()
    for c in copies:
        c.wait()


def fetch(x, after):
    parts = max(p for p in range(1, 9) if x.shape[0] % (16 * p) == 0)
    size = x.size * x.dtype.itemsize
    return pl.pallas_call(
        functools.partial(fetch_kernel, parts),
        in_specs=[pl.BlockSpec(memory_space=pl.ANY)] * 2,
        out_specs=LOCAL,
        out_shape=pltpu.VMEM(x.shape, x.dtype),
        scratch_shapes=[pltpu.SemaphoreType.DMA((parts,))],
        compiler_params=params(1024 * 1024),
        cost_estimate=SHORT,
        name="fetch",
    )(pltpu.with_memory_space_constraint(x, pltpu.HBM), after)


def spans(size, want):
    return [(at, min(want, size - at)) for at in range(0, size, want)]


def expert_kernel(blocks, slots, expert_ref, *refs):
    half = blocks // 2
    block_refs, refs = refs[:blocks], refs[blocks:]
    weight_refs, refs = refs[:3], refs[3:]
    own_refs, other_ref, refs = refs[:half], refs[half], refs[half + 1 :]
    table, hidden, weighted, *weights, sems = refs
    rows = block_refs[0].shape[0]
    width, units = weight_refs[0].shape
    count = blocks * rows
    cuts = [spans(units, CUT), spans(units, CUT), spans(width, DOWN_CUT)]
    waits = [[] for _ in range(3)]

    def load(w, j):
        at, size = cuts[w][j]
        c = pltpu.make_async_copy(
            weight_refs[w].at[:, pl.ds(at, size)],
            weights[w].at[:, pl.ds(at, size)],
            sems.at[w, j],
        )
        c.start()
        waits[w].append(c)

    for j in range(len(cuts[0])):
        load(0, j)
        load(1, j)
    for j in range(len(cuts[2])):
        load(2, j)
    for i, ref in enumerate(block_refs):
        table[i * rows : (i + 1) * rows, :] = ref[...]
    own = expert_ref[0].astype(F32)
    meta = jnp.transpose(table[:, width:].astype(F32))
    first = meta[0:1] == own
    second = meta[4:5] == own
    member = jnp.logical_or(first, second)
    weight = jnp.where(first, meta[1:2] + meta[2:3] + meta[3:4], meta[5:6] + meta[6:7] + meta[7:8])
    flag = jnp.where(member, 1.0, 0.0)
    part = min(count, 512)
    before = lax.broadcasted_iota(jnp.int32, (part, part), 0) < lax.broadcasted_iota(
        jnp.int32, (part, part), 1
    )
    before = jnp.where(before, 1.0, 0.0).astype(BF16)
    ranks, base = [], jnp.zeros((1, 1), F32)
    for at in range(0, count, part):
        some = flag[:, at : at + part]
        rank = jnp.dot(
            jnp.broadcast_to(some, (8, part)).astype(BF16), before, preferred_element_type=F32
        )
        ranks.append(rank[0:1] + base)
        base = base + jnp.sum(some, axis=1, keepdims=True)
    rank = jnp.where(member, jnp.concatenate(ranks, axis=1), -1.0).astype(jnp.int32)
    chosen = lax.broadcasted_iota(jnp.int32, (slots, count), 0) == rank
    place = jnp.where(chosen, 1.0, 0.0).astype(BF16)
    scale = jnp.sum(jnp.where(chosen, weight, 0.0), axis=1, keepdims=True)
    x = jnp.dot(place, table[:, :width], preferred_element_type=F32).astype(BF16)
    back = jnp.transpose(place)
    for j, (start, size) in enumerate(cuts[0]):
        waits[0][j].wait()
        waits[1][j].wait()
        for at, some in spans(size, 256):
            at = slice(start + at, start + at + some)
            g = jnp.dot(x, weights[0][:, at], preferred_element_type=F32)
            u = jnp.dot(x, weights[1][:, at], preferred_element_type=F32)
            hidden[:, at] = (g / (1.0 + jnp.exp(-g)) * u).astype(BF16)
    ready = 0
    for j, (start, size) in enumerate(cuts[2]):
        waits[2][j].wait()
        for at, some in spans(size, 256):
            at = slice(start + at, start + at + some)
            y = jnp.dot(hidden[...], weights[2][:, at], preferred_element_type=F32)
            weighted[:, at] = (y * scale).astype(BF16)
        end = start + size
        if end - ready < SPREAD and end < width:
            continue
        at = slice(ready, end)
        spread = jnp.dot(back, weighted[:, at], preferred_element_type=F32).astype(BF16)
        for i, ref in enumerate(own_refs):
            ref[:, at] = spread[i * rows : (i + 1) * rows]
        other_ref[:, at] = spread[half * rows :]
        ready = end


def run_expert(expert, block_list, weights, cap):
    blocks = len(block_list)
    rows = block_list[0].shape[0]
    width, units = weights[0].shape
    slots = blocks * cap
    count = blocks * rows
    half = blocks // 2
    cuts = max(len(spans(units, CUT)), len(spans(width, DOWN_CUT)))
    return pl.pallas_call(
        functools.partial(expert_kernel, blocks, slots),
        in_specs=[pl.BlockSpec(memory_space=pltpu.SMEM)]
        + [LOCAL] * blocks
        + [pl.BlockSpec(memory_space=pl.ANY)] * 3,
        out_specs=[LOCAL] * (half + 1),
        out_shape=[jax.ShapeDtypeStruct((rows, width), BF16)] * half
        + [jax.ShapeDtypeStruct((half * rows, width), BF16)],
        scratch_shapes=[
            pltpu.VMEM((count, width + META), BF16),
            pltpu.VMEM((slots, units), BF16),
            pltpu.VMEM((slots, width), BF16),
            *(pltpu.VMEM(w.shape, BF16) for w in weights),
            pltpu.SemaphoreType.DMA((3, cuts)),
        ],
        compiler_params=params(6 * width * units + 10 * count * (width + META)),
        cost_estimate=SHORT,
        name="expert",
    )(expert, *map(near_core, block_list), *map(in_hbm, weights))


def add_kernel(count, rows, *refs):
    own, other, out = refs[:count], refs[count:-count], refs[-count:]
    for i in range(count):
        got = other[0][i * rows : (i + 1) * rows] if len(other) == 1 else other[i][...]
        out[i][...] = (own[i][...].astype(F32) + got.astype(F32)).astype(BF16)


def add_blocks(own, other):
    count = len(own)
    rows, width = own[0].shape
    return pl.pallas_call(
        functools.partial(add_kernel, count, rows),
        in_specs=[LOCAL] * (count + len(other)),
        out_specs=[LOCAL] * count,
        out_shape=[jax.ShapeDtypeStruct((rows, width), BF16)] * count,
        compiler_params=params(12 * count * rows * width),
        cost_estimate=SHORT,
        name="add_blocks",
    )(*own, *other)


def finish_kernel(parts, lengths_ref, tokens_ref, gain_ref, *refs):
    hidden_ref, normed_ref, norm_ref = refs[parts:]
    total = refs[0][...].astype(F32)
    for ref in refs[1:parts]:
        total = total + ref[...].astype(F32)
    hidden = (tokens_ref[...].astype(F32) + total).astype(BF16)
    hidden_ref[...] = hidden
    wide = hidden.astype(F32)
    width = wide.shape[1]
    square = jnp.sum(wide * wide, axis=1, keepdims=True)
    normed_ref[...] = (wide * lax.rsqrt(square / width + norm_eps) * gain_ref[...]).astype(BF16)
    row = lax.broadcasted_iota(jnp.int32, square.shape, 0)
    lane = lax.broadcasted_iota(jnp.int32, norm_ref.shape, 1)
    out, start = jnp.zeros(norm_ref.shape, F32), 0
    for j in range(norm_ref.shape[1]):
        end = start + lengths_ref[0, j]
        member = jnp.logical_and(row >= start, row < end)
        mean = jnp.sum(jnp.where(member, square, 0.0), axis=0, keepdims=True) / (
            lengths_ref[0, j].astype(F32) * width
        )
        out = jnp.where(lane == j, jnp.sqrt(mean), out)
        start = end
    norm_ref[...] = out


def finish(lengths, tokens, gain, parts):
    rows, width = tokens.shape
    return pl.pallas_call(
        functools.partial(finish_kernel, len(parts)),
        in_specs=[pl.BlockSpec(memory_space=pltpu.SMEM)] + [LOCAL] * (2 + len(parts)),
        out_specs=[LOCAL] * 3,
        out_shape=[
            jax.ShapeDtypeStruct((rows, width), BF16),
            jax.ShapeDtypeStruct((rows, width), BF16),
            jax.ShapeDtypeStruct(lengths.shape, F32),
        ],
        compiler_params=params(8 * 1024 * 1024),
        name="finish",
    )(lengths, tokens, gain, *parts)


def request_kernel(lengths_ref, *refs):
    out_ref = refs[-1]
    peak = refs[0][...]
    for ref in refs[1:-1]:
        peak = jnp.maximum(peak, ref[...])
    row = lax.broadcasted_iota(jnp.int32, peak.shape, 1)
    lane = lax.broadcasted_iota(jnp.int32, out_ref.shape, 1)
    out, start = jnp.zeros(out_ref.shape, F32), 0
    for j in range(out_ref.shape[1]):
        end = start + lengths_ref[0, j]
        member = jnp.logical_and(row >= start, row < end)
        best = jnp.max(jnp.where(member, peak, -jnp.inf), axis=1, keepdims=True)
        out = jnp.where(lane == j, best, out)
        start = end
    out_ref[...] = out


def request_peaks(lengths, found):
    return pl.pallas_call(
        request_kernel,
        in_specs=[pl.BlockSpec(memory_space=pltpu.SMEM)] + [LOCAL] * len(found),
        out_specs=LOCAL,
        out_shape=jax.ShapeDtypeStruct(lengths.shape, F32),
        compiler_params=params(1024 * 1024),
        name="request_peaks",
    )(lengths, *found)


def peak_kernel(blocks, start, stop, *refs):
    block_refs = refs[:blocks]
    head_ref, *prior, out_ref, table = refs[blocks:]
    rows = block_refs[0].shape[0]
    for i, ref in enumerate(block_refs):
        table[i * rows : (i + 1) * rows, :] = ref[...]
    words = stop - start
    tile = max(t for t in range(16, 513, 16) if words % t == 0)
    best = None
    for at in range(start, stop, tile):
        logits = lax.dot_general(
            head_ref[at : at + tile, :],
            table[...],
            (((1,), (1,)), ((), ())),
            preferred_element_type=F32,
        )
        peak = jnp.max(logits, axis=0, keepdims=True)
        best = peak if best is None else jnp.maximum(best, peak)
    for i in range(blocks):
        line = best[:, i * rows : (i + 1) * rows]
        if prior:
            line = jnp.maximum(line, prior[0][i : i + 1, :])
        out_ref[i : i + 1, :] = line


def peaks(block_list, words_first, start, stop, prior=()):
    blocks = len(block_list)
    rows, width = block_list[0].shape
    return pl.pallas_call(
        functools.partial(peak_kernel, blocks, start, stop),
        in_specs=[LOCAL] * (blocks + 1 + len(prior)),
        out_specs=LOCAL,
        out_shape=jax.ShapeDtypeStruct((blocks, rows), F32),
        scratch_shapes=[pltpu.VMEM((blocks * rows, width), BF16)],
        compiler_params=params(12 * 1024 * 1024),
        cost_estimate=SHORT,
        name="peaks",
    )(*map(near_core, block_list), near_core(words_first), *prior)


def per_device(
    n_req,
    n_exp,
    tokens,
    routes,
    router,
    gate_weight,
    up_weight,
    down_weight,
    norm_gain,
    head_weight,
    lengths,
):
    row_count, width = tokens.shape
    experts = router.shape[1]
    half_exp = n_exp // 2
    group_size = n_req * n_exp // (2 * experts)
    r = lax.axis_index("req")
    e = lax.axis_index("exp")
    expert = ((r * half_exp + e % half_exp) // group_size).astype(jnp.int32).reshape(1)

    def send(x, flips0, flips1=None):
        pairs = flip_pairs(n_req, n_exp, (flips0, flips0 if flips1 is None else flips1))
        return lax.ppermute(x, AXES, pairs)

    core = [("req", 1)]
    dims = [("req", b) for b in bits_below(n_req, 2)] + [("exp", b) for b in bits_below(half_exp)]
    extra, dims = dims[3:], dims[:3]
    turned = dims[1:] + dims[:1]

    def hop(x, *js):
        return send(x, [dims[j] for j in js], [turned[j] for j in js])

    block = prepare(tokens, routes, router)
    for d in extra:
        block = jnp.concatenate([block, send(block, [d])], axis=0)
    near = [block, hop(block, 0)]
    near += [hop(b, 1) for b in near]
    far = [hop(b, 2) for b in near]
    near += [send(b, core) for b in near]
    cap = CAP * block.shape[0] // row_count
    rows = block.shape[0]

    weights = [gate_weight, up_weight, down_weight]
    *near_out, near_other = run_expert(expert, near, weights, cap)
    far, near_out = lax.optimization_barrier((far, near_out))
    far += [send(b, core) for b in far]
    *far_out, far_other = run_expert(expert, far, weights, cap)
    words_first = fetch(head_weight.T, far_other)
    far_sum = add_blocks(far_out, [send(far_other, core)])
    f3 = hop(far_sum[3], 1)
    f2 = hop(far_sum[2], 1)
    f1 = hop(add_blocks([far_sum[1]], [f3])[0], 0, 2)
    f0 = hop(add_blocks([far_sum[0]], [f2])[0], 2)
    near_sum = add_blocks(near_out, [send(near_other, core)])
    n3 = hop(near_sum[3], 1)
    n2 = hop(near_sum[2], 1)
    n1 = hop(add_blocks([near_sum[1]], [n3])[0], 0)
    parts = [near_sum[0], n2, n1, f0, f1]
    for d in reversed(extra):
        merged = sum(p.astype(F32) for p in parts).astype(BF16)
        size = merged.shape[0] // 2
        parts = [merged[:size], send(merged[size:], [d])]
    parts, words_first = lax.optimization_barrier((parts, words_first))
    hidden_out, normed, request_norm = finish(lengths, tokens, norm_gain.reshape(1, width), parts)

    exp_dims = [("exp", b) for b in bits_below(half_exp)]
    across = ("exp", half_exp)

    def tree(dims0, dims1):
        ways = [([], [])]
        for p, q in zip(dims0, dims1):
            ways += [(a + [p], b + [q]) for a, b in ways]
        return ways

    def give_back(group, peak):
        out = []
        for n, (side, i) in enumerate(group):
            p, q = trees[side][i]
            one = peak[n : n + 1]
            if side:
                one = send(one, p + [across], q + [across])
            elif p:
                one = send(one, p, q)
            out.append(one)
        return out

    trees = tree(exp_dims[::-1], exp_dims[::-1]), tree(exp_dims[1:] + exp_dims[:1], exp_dims)
    singles = [i for i, (p, _) in enumerate(trees[0]) if len(p) == 1]
    first = send(normed, [across])
    first, *near_singles = lax.optimization_barrier(
        (first, *(send(normed, *trees[0][i]) for i in singles))
    )
    held = {(0, 0): normed, (1, 0): first}
    for i, x in zip(singles, near_singles):
        held[0, i] = x
        held[1, i] = send(first, *trees[1][i])
    early = sorted(k for k in held if k == (1, 0) or k[0] == 0)
    words = head_weight.shape[1]
    cut = words // 32 * 16
    early_in = [held[k] for k in early]
    peak = peaks(early_in, words_first, 0, cut)
    for i in singles:
        held[1, i], peak = lax.optimization_barrier((held[1, i], peak))
    for side in (0, 1):
        for i, (p, q) in enumerate(trees[side]):
            if len(p) > 1:
                before = trees[side].index((p[:-1], q[:-1]))
                held[side, i] = send(held[side, before], p[-1:], q[-1:])
    peak = peaks(early_in, words_first, cut, words, [peak])
    late = sorted((k for k in held if k not in early), reverse=True)
    found = give_back(early, peak)
    found += give_back(late, peaks([held[k] for k in late], words_first, 0, words))
    request_max = request_peaks(lengths, found)
    return (hidden_out, request_norm[0], request_max[0])


def solution(mesh):
    placed = (
        P(AXES, None),
        P(AXES, None),
        P(),
        P(None, AXES),
        P(None, AXES),
        P(AXES, None),
        P(),
        P(None, "exp"),
        P(AXES, None),
    )
    return jax.shard_map(
        functools.partial(per_device, mesh.shape["req"], mesh.shape["exp"]),
        mesh=mesh,
        in_specs=placed,
        out_specs=(P(AXES, None), P(AXES), P(AXES)),
        check_vma=False,
    )
```
